256 devices in a mesh: ctx: 64 (over z_lo, y, x), head: 4 (over z_hi, core).
Axes of the slice: x: 4, y: 4, z: 8 (z_hi: 2, z_lo: 4; z = z_hi * 4 + z_lo), core: 2. Of those that a mesh axis runs over, the one named last changes fastest.
Arguments:
- q_latent: bfloat16 [8192, 64, 512], P('ctx', 'head'), may hold values from -52 to 52
- q_rope: bfloat16 [8192, 4096], P('ctx', 'head'), may hold values from -6 to 6
- kv_latent: bfloat16 [8192, 512], P('ctx'), may hold values from -4 to 4
- k_rope: bfloat16 [8192, 64], P('ctx'), may hold values from -4 to 4
- out_grad: bfloat16 [8192, 64, 512], P('ctx', 'head'), may hold values from -6 to 6
- block_pos: int32 [128], replicated, may hold values from 0 to 127, each once
Outputs:
- grad_q_latent: bfloat16 [8192, 64, 512], P('ctx', 'head')
- grad_q_rope: bfloat16 [8192, 4096], P('ctx', 'head')
- grad_kv_latent: bfloat16 [8192, 512], P(('ctx', 'head'))
- grad_k_rope: bfloat16 [8192, 64], P(('ctx', 'head'))
The draws below stay inside these ranges and needn't reach their ends.
Inputs may be any that keep to these rules, and one draw needn't show every extreme that they name: `block_pos`: each of the 128 context blocks appears once.
All inputs are finite; a program needn't handle non-finite values.
Results may differ from the reference program's by a relative error of at most 0.017.
Values may be sent and summed in bfloat16 or wider, within the bound.
A program may use at most 128 MiB of HBM per device.

```python
import jax
import jax.numpy as jnp
from jax import lax

LAT = 512
ROPE = 64
HEADS = 64
SPAN = 4
BLOCK = 64
BLOCKS = 128
TOKENS = 8192
N_CTX = 64


def base_keys(key):
    latent = jnp.clip(jax.random.normal(jax.random.fold_in(key, 101), (TOKENS, LAT), jnp.float32), -4.0, 4.0)
    rotary = jnp.clip(jax.random.normal(jax.random.fold_in(key, 102), (TOKENS, ROPE), jnp.float32), -4.0, 4.0)
    return (latent, rotary)


def draw_kv_latent(key, part):
    latent, rotary = base_keys(key)
    return latent.astype(jnp.bfloat16)


def draw_k_rope(key, part):
    latent, rotary = base_keys(key)
    return rotary.astype(jnp.bfloat16)


def draw_q_latent(key, part):
    key = jax.random.fold_in(key, 3)
    return jnp.clip(jax.random.normal(key, (TOKENS, HEADS, LAT), jnp.float32), -6.0, 6.0).astype(jnp.bfloat16)


def levels(stream_key, dims, split, smallest, top_value):
    level = 1.0
    for dim, shards_of in split:
        steps = jax.random.uniform(jax.random.fold_in(jax.random.fold_in(stream_key, 6), dim), (shards_of,), jnp.float32, smallest / len(split), top_value / len(split))
        level = level * jnp.repeat(jnp.exp(steps), dims[dim] // shards_of).reshape((-1,) + (1,) * (len(dims) - 1 - dim))
    return level


def centred(stream_key, extent, deviation, reach, cuts=(), kind=jnp.bfloat16):
    entries = jax.random.normal(stream_key, extent, jnp.float32) * deviation
    if len(cuts) > 0:
        entries = levels(stream_key, extent, cuts, -0.22, 0.18) * entries
    return jnp.clip(entries, min=-reach, max=reach).astype(kind)


def setup_inputs(seed: int = 0) -> dict:
    splits = jax.random.split(jax.random.key(seed), 7)
    return {
        "q_latent": draw_q_latent(jax.random.fold_in(splits[6], 71), 0),
        "q_rope": centred(splits[1], (TOKENS, HEADS * ROPE), 1.0, 6.0, ((0, 64), (1, 4))),
        "kv_latent": draw_kv_latent(jax.random.fold_in(splits[6], 71), 0),
        "k_rope": draw_k_rope(jax.random.fold_in(splits[6], 71), 0),
        "out_grad": centred(splits[4], (TOKENS, HEADS, LAT), 1.0, 6.0, ((0, 64), (1, 4))),
        "block_pos": jax.random.permutation(splits[5], BLOCKS).astype(jnp.int32),
    }


SCALE = 192.0 ** -0.5


def reference(q_latent, q_rope, kv_latent, k_rope, out_grad, block_pos):
    span_tokens = 2 * BLOCK
    offsets = jnp.arange(BLOCK, dtype=jnp.int32)
    all_pos = (block_pos[:, None] * BLOCK + offsets[None, :]).reshape(TOKENS).astype(jnp.int32)
    q_rot_all = q_rope.reshape(TOKENS, HEADS, ROPE)

    def rows(array, device):
        start = (device * span_tokens).astype(jnp.int32)
        return lax.dynamic_slice_in_dim(array, start, span_tokens, 0)

    def one(carry, device):
        grad_lat, grad_rot = carry
        q_lat = rows(q_latent, device).astype(jnp.float32)
        q_rot = rows(q_rot_all, device).astype(jnp.float32)
        grad_out = rows(out_grad, device).astype(jnp.float32)
        query_pos = rows(all_pos, device)
        sources = [((device - step) % N_CTX).astype(jnp.int32) for step in range(SPAN)]
        key_lat = jnp.concatenate([rows(kv_latent, s) for s in sources], 0).astype(jnp.float32)
        key_rot = jnp.concatenate([rows(k_rope, s) for s in sources], 0).astype(jnp.float32)
        key_pos = jnp.concatenate([rows(all_pos, s) for s in sources], 0)
        latent_part = jnp.einsum("thl,kl->thk", q_lat, key_lat)
        rot_part = jnp.einsum("thr,kr->thk", q_rot, key_rot)
        scores = SCALE * (latent_part + rot_part)
        visible = key_pos[None, None, :] <= query_pos[:, None, None]
        scores = jnp.where(visible, scores, -jnp.inf)
        top = jnp.max(scores, axis=-1, keepdims=True)
        expo = jnp.exp(scores - top)
        probs = expo / jnp.sum(expo, axis=-1, keepdims=True)
        weights = lax.optimization_barrier(probs.astype(jnp.bfloat16)).astype(jnp.float32)
        output = jnp.einsum("thk,kl->thl", weights, key_lat)
        delta = jnp.sum(grad_out * output, axis=-1)
        grad_probs = jnp.einsum("thl,kl->thk", grad_out, key_lat)
        grad_scores = probs * (grad_probs - delta[:, :, None])
        grad_scores = lax.optimization_barrier(grad_scores.astype(jnp.bfloat16)).astype(jnp.float32)
        dq_lat = SCALE * jnp.einsum("thk,kl->thl", grad_scores, key_lat)
        dq_rot = SCALE * jnp.einsum("thk,kr->thr", grad_scores, key_rot)
        key_grad_lat = SCALE * jnp.einsum("thk,thl->kl", grad_scores, q_lat) + jnp.einsum("thk,thl->kl", weights, grad_out)
        key_grad_rot = SCALE * jnp.einsum("thk,thr->kr", grad_scores, q_rot)
        for step in range(SPAN):
            start = (sources[step] * span_tokens).astype(jnp.int32)
            piece_lat = key_grad_lat[step * span_tokens:(step + 1) * span_tokens]
            piece_rot = key_grad_rot[step * span_tokens:(step + 1) * span_tokens]
            grad_lat = lax.dynamic_update_slice_in_dim(grad_lat, lax.dynamic_slice_in_dim(grad_lat, start, span_tokens, 0) + piece_lat, start, 0)
            grad_rot = lax.dynamic_update_slice_in_dim(grad_rot, lax.dynamic_slice_in_dim(grad_rot, start, span_tokens, 0) + piece_rot, start, 0)
        return (grad_lat, grad_rot), (dq_lat.astype(jnp.bfloat16), dq_rot.reshape(span_tokens, HEADS * ROPE).astype(jnp.bfloat16))

    init = (jnp.zeros((TOKENS, LAT), jnp.float32), jnp.zeros((TOKENS, ROPE), jnp.float32))
    (grad_lat, grad_rot), (dq_lat, dq_rot) = lax.scan(one, init, jnp.arange(N_CTX, dtype=jnp.int32))
    return (dq_lat.reshape(TOKENS, HEADS, LAT), dq_rot.reshape(TOKENS, HEADS * ROPE), grad_lat.astype(jnp.bfloat16), grad_rot.astype(jnp.bfloat16))
```

```python
import functools

import jax
import jax.numpy as jnp
from jax import lax
from jax.experimental import pallas as pl
from jax.experimental.pallas import tpu as pltpu
from jax.sharding import PartitionSpec as P

SPAN = 4
LAT = 512
ROPE = 64
WIDE = 640
SCALE = 192.0 ** (-0.5)
SCALE_LOG2 = SCALE * 1.4426950408889634
CHUNK = 256
SPLITS = ((256, 384), (0, 256))

NT = (((1,), (1,)), ((), ()))
TN = (((0,), (0,)), ((), ()))


def dot(a, b, dims=(((1,), (0,)), ((), ()))):
    return lax.dot_general(a, b, dims, preferred_element_type=jnp.float32)


def kernel(
    n_ctx, heads,
    block_pos, kv_ref, kr_ref, qr_ref, q_hbm, g_hbm,
    dq_hbm, dqr_ref, dkv_ref, dkr_ref,
    kvr, qv, gv, rot32, s_a, s_b, dp_a, dp_b, ds_t, w_t, dq_st,
    d0, d1, as0, as1, ar0, ar1, bs0, bs1, br0, br1, cs0, cs1, cr0, cr1,
    in_sem, out_sem, f_send, f_recv, p_send, p_recv,
    a_send, a_recv, b_send, b_recv, c_send, c_recv,
):
    c = lax.axis_index("ctx")
    h = lax.axis_index("head")
    z = lax.div(h, 2)
    a = lax.rem(h, 2)
    sib = z * 2 + (1 - a)
    zpart = (1 - z) * 2 + a
    rows = qv.shape[0]
    n_chunks = rows // CHUNK
    half = rows // 2

    def ctx_at(k):
        return lax.rem(c + k + n_ctx, n_ctx)

    loads = [
        pltpu.make_async_copy(q_hbm, qv.at[:, pl.ds(0, LAT)], in_sem.at[0]),
        pltpu.make_async_copy(g_hbm, gv, in_sem.at[1]),
    ]
    for load in loads:
        load.start()

    barrier = pltpu.get_barrier_semaphore()
    peers = [(ctx_at(k), h) for k in (1, 2, 3, -1, -2, -3)] + [(c, sib), (c, zpart)]
    for peer in peers:
        pl.semaphore_signal(barrier, inc=1, device_id=peer, device_id_type=pl.DeviceIdType.MESH)

    kvr[0, :, :, pl.ds(0, LAT)] = kv_ref[...].reshape(2, 64, LAT)
    kvr[0, :, :, pl.ds(LAT, 128)] = jnp.concatenate(
        [kr_ref[...], jnp.zeros_like(kr_ref[...])], axis=1
    ).reshape(2, 64, 128)

    pl.semaphore_wait(barrier, len(peers))

    def remote(src, dst, send, recv, peer):
        return pltpu.make_async_remote_copy(
            src_ref=src, dst_ref=dst, send_sem=send, recv_sem=recv,
            device_id=peer, device_id_type=pl.DeviceIdType.MESH,
        )

    forward = {}
    for k in (2, 1, 3):
        forward[k] = remote(
            kvr.at[0, a], kvr.at[k, a], f_send.at[k - 1], f_recv.at[k - 1], (ctx_at(k), h)
        )
        forward[k].start()

    tokens = qr_ref.shape[0]
    low = lax.broadcasted_iota(jnp.int32, (tokens, 128), 1) < ROPE
    for j in range(heads // 2):
        tile = qr_ref[:, pl.ds(j * 128, 128)].astype(jnp.float32)
        rot32[pl.ds(2 * j, tokens, stride=heads), :] = jnp.where(low, tile, 0.0)
        rot32[pl.ds(2 * j + 1, tokens, stride=heads), :] = jnp.where(
            low, pltpu.roll(tile, 64, 1), 0.0
        )
    qv[:, pl.ds(LAT, 128)] = rot32[...].astype(jnp.bfloat16)

    passed = {}
    for k in (1, 3, 2):
        forward[k].wait_recv()
        passed[k] = remote(
            kvr.at[k, a], kvr.at[k, a], p_send.at[k - 1], p_recv.at[k - 1], (c, sib)
        )
        passed[k].start()
    for load in loads:
        load.wait()
    for k in (1, 3, 2):
        passed[k].wait_recv()

    key_pos = [
        block_pos[2 * ctx_at(-(slot // 2)) + slot % 2] for slot in range(2 * SPAN)
    ]
    query_pos = [block_pos[2 * c], block_pos[2 * c + 1]]

    def score(start, s_buf, dp_buf):
        at = pl.ds(start, CHUNK)
        keys = kvr[...].reshape(SPAN * 128, WIDE)
        s_buf[...] = dot(keys, qv[at, :], NT)
        dp_buf[...] = dot(keys[:, :LAT], gv[at, :], NT)

    lane_row = lax.broadcasted_iota(jnp.int32, (64, CHUNK), 1)
    sub_row = lax.broadcasted_iota(jnp.int32, (64, CHUNK), 0)

    def soften(start, s_buf, dp_buf):
        at = pl.ds(start, CHUNK)
        second = start // half
        pos = query_pos[second] * 64
        ahead = lax.div(lane_row + (start - second * half), heads) - sub_row
        top = None
        for slot in range(2 * SPAN):
            part = pl.ds(slot * 64, 64)
            seen = ahead >= key_pos[slot] * 64 - pos
            s = jnp.where(seen, s_buf[part, :], -jnp.inf)
            s_buf[part, :] = s
            m = jnp.max(s, axis=0, keepdims=True)
            top = m if top is None else jnp.maximum(top, m)
        total = None
        for slot in range(2 * SPAN):
            part = pl.ds(slot * 64, 64)
            e = jnp.exp2((s_buf[part, :] - top) * SCALE_LOG2)
            s_buf[part, :] = e
            t = jnp.sum(e, axis=0, keepdims=True)
            total = t if total is None else total + t
        inv = 1.0 / total
        delta = None
        for slot in range(2 * SPAN):
            part = pl.ds(slot * 64, 64)
            w = (s_buf[part, :] * inv).astype(jnp.bfloat16)
            w_t[part, at] = w
            t = jnp.sum(w.astype(jnp.float32) * dp_buf[part, :], axis=0, keepdims=True)
            delta = t if delta is None else delta + t
        for slot in range(2 * SPAN):
            part = pl.ds(slot * 64, 64)
            ds_t[part, at] = (
                (s_buf[part, :] * inv) * (dp_buf[part, :] - delta)
            ).astype(jnp.bfloat16)

    score(0, s_a, dp_a)

    def pair(i, _):
        start = i * (2 * CHUNK)
        score(start + CHUNK, s_b, dp_b)
        soften(start, s_a, dp_a)
        score((start + 2 * CHUNK) % rows, s_a, dp_a)
        soften(start + CHUNK, s_b, dp_b)
        return 0

    for i in range(n_chunks // 2):
        pair(i, 0)

    d, asb, arb, bsb, brb = (d0, d1), (as0, as1), (ar0, ar1), (bs0, bs1), (br0, br1)
    csb, crb = (cs0, cs1), (cr0, cr1)

    def key_grads(n):
        first, width = SPLITS[n]
        shape = (2 * SPAN, 2, 32, width)
        part = SCALE * dot(ds_t[...], qv[:, pl.ds(first, width)])
        latent = min(width, LAT - first)
        other = dot(w_t[...], gv[:, pl.ds(first, latent)])
        if latent == width:
            d[n][...] = (part + other).reshape(shape)
        else:
            d[n][:, :, :, pl.ds(0, latent)] = (part[:, :latent] + other).reshape(shape[:3] + (latent,))
            d[n][:, :, :, pl.ds(latent, width - latent)] = part[:, latent:].reshape(
                shape[:3] + (width - latent,)
            )
        asb[n][...] = d[n][:, pl.ds(1 - a, 1)].reshape(2 * SPAN, 32, width).astype(jnp.bfloat16)
        copy = remote(asb[n], arb[n], a_send.at[n], a_recv.at[n], (c, sib))
        copy.start()
        return copy

    def own(n, k):
        width = SPLITS[n][1]
        return d[n][pl.ds(2 * k, 2), pl.ds(a, 1)].reshape(2, 32, width)

    def add_cores(n, copy):
        copy.wait_recv()
        sends = []
        for k in (2, 1, 3):
            got = arb[n][pl.ds(2 * k, 2)].astype(jnp.float32)
            bsb[n][k - 1] = (own(n, k) + got).astype(jnp.bfloat16)
            sends.append(remote(
                bsb[n].at[k - 1], brb[n].at[k - 1], b_send.at[n, k - 1], b_recv.at[n, k - 1],
                (ctx_at(-k), h),
            ))
            sends[-1].start()
        return sends

    def add_context(n, sends):
        for copy in sends:
            copy.wait_recv()
        sums = own(n, 0) + arb[n][pl.ds(0, 2)].astype(jnp.float32)
        for k in (1, 2, 3):
            sums = sums + brb[n][k - 1].astype(jnp.float32)
        width = SPLITS[n][1]
        d[n][pl.ds(0, 2), pl.ds(a, 1)] = sums.reshape(2, 1, 32, width)
        csb[n][...] = d[n][pl.ds(1 - z, 1), pl.ds(a, 1)].reshape(32, width).astype(jnp.bfloat16)
        copy = remote(csb[n], crb[n], c_send.at[n], c_recv.at[n], (c, zpart))
        copy.start()
        return copy

    def finish(n, copy):
        copy.wait_recv()
        first, width = SPLITS[n]
        result = d[n][pl.ds(z, 1), pl.ds(a, 1)].reshape(32, width) + crb[n][...].astype(jnp.float32)
        result = result.astype(jnp.bfloat16)
        latent = min(width, LAT - first)
        dkv_ref[:, pl.ds(first, latent)] = result[:, :latent]
        if latent < width:
            dkr_ref[...] = result[:, latent:latent + ROPE]

    def query_grads(i):
        start = i * CHUNK
        at = pl.ds(start, CHUNK)
        keys = kvr[...].reshape(SPAN * 128, WIDE)
        grad = SCALE * dot(ds_t[:, at], keys, TN)
        dq_st[at, :] = grad[:, :LAT].astype(jnp.bfloat16)
        rot32[at, :] = grad[:, LAT:]

    def store(i):
        at = pl.ds(i * CHUNK, CHUNK)
        return pltpu.make_async_copy(dq_st.at[at, :], dq_hbm.at[at, :], out_sem.at[i])

    stores = []

    def query_step(i):
        query_grads(i)
        stores.append(store(i))
        stores[-1].start()

    a0 = key_grads(0)
    a1 = key_grads(1)
    b0 = add_cores(0, a0)
    query_step(0)
    query_step(1)
    b1 = add_cores(1, a1)
    query_step(2)
    query_step(3)
    query_step(4)
    c0 = add_context(0, b0)
    query_step(5)
    query_step(6)
    query_step(7)

    for j in range(heads // 2):
        even = rot32[pl.ds(2 * j, tokens, stride=heads), :]
        odd = rot32[pl.ds(2 * j + 1, tokens, stride=heads), :]
        dqr_ref[:, pl.ds(j * 128, 128)] = jnp.where(
            low, even, pltpu.roll(odd, 64, 1)
        ).astype(jnp.bfloat16)

    c1 = add_context(1, b1)
    finish(0, c0)
    for copy in [*forward.values(), *passed.values(), a0, a1, *b0, *b1, c0]:
        copy.wait_send()
    for copy in stores:
        copy.wait()
    finish(1, c1)
    c1.wait_send()


def per_device(q_latent, q_rope, kv_latent, k_rope, out_grad, block_pos):
    tokens, heads, lat = q_latent.shape
    rows = tokens * heads
    keys = SPAN * tokens
    n_ctx = lax.axis_size("ctx")
    bf16, f32 = jnp.bfloat16, jnp.float32
    vmem = pl.BlockSpec(memory_space=pltpu.VMEM)
    hbm = pl.BlockSpec(memory_space=pl.ANY)
    smem = pl.BlockSpec(memory_space=pltpu.SMEM)
    widths = [width for _, width in SPLITS]

    def pairs(shape, kind):
        return [pltpu.VMEM(shape + (width,), kind) for width in widths]

    dma = pltpu.SemaphoreType.DMA
    scratch = [
        pltpu.VMEM((SPAN, 2, 64, WIDE), bf16),
        pltpu.VMEM((rows, WIDE), bf16),
        pltpu.VMEM((rows, lat), bf16),
        pltpu.VMEM((rows, 128), f32),
        *[pltpu.VMEM((keys, CHUNK), f32) for _ in range(4)],
        pltpu.VMEM((keys, rows), bf16),
        pltpu.VMEM((keys, rows), bf16),
        pltpu.VMEM((rows, lat), bf16),
        *pairs((2 * SPAN, 2, 32), f32),
        *pairs((2 * SPAN, 32), bf16),
        *pairs((2 * SPAN, 32), bf16),
        *pairs((3, 2, 32), bf16),
        *pairs((3, 2, 32), bf16),
        *pairs((32,), bf16),
        *pairs((32,), bf16),
        dma((2,)), dma((rows // CHUNK,)),
        dma((3,)), dma((3,)), dma((3,)), dma((3,)),
        dma((2,)), dma((2,)), dma((2, 3)), dma((2, 3)), dma((2,)), dma((2,)),
    ]
    macs = rows * keys * (WIDE * 3 + 2 * lat)
    dq, dqr, dkv, dkr = pl.pallas_call(
        functools.partial(kernel, n_ctx, heads),
        out_shape=(
            jax.ShapeDtypeStruct((rows, lat), bf16),
            jax.ShapeDtypeStruct((tokens, heads * ROPE), bf16),
            jax.ShapeDtypeStruct((tokens // 4, lat), bf16),
            jax.ShapeDtypeStruct((tokens // 4, ROPE), bf16),
        ),
        in_specs=[smem, vmem, vmem, vmem, hbm, hbm],
        out_specs=(hbm, vmem, vmem, vmem),
        scratch_shapes=scratch,
        compiler_params=pltpu.CompilerParams(
            collective_id=0, has_side_effects=True, vmem_limit_bytes=48 * 2**20
        ),
        cost_estimate=pl.CostEstimate(
            flops=2 * macs, bytes_accessed=7 * 2**20, transcendentals=rows * keys
        ),
    )(
        block_pos, kv_latent, k_rope, q_rope,
        q_latent.reshape(rows, lat), out_grad.reshape(rows, lat),
    )
    return dq.reshape(tokens, heads, lat), dqr, dkv, dkr


def solution(mesh):
    in_specs = (
        P("ctx", "head", None),
        P("ctx", "head"),
        P("ctx", None),
        P("ctx", None),
        P("ctx", "head", None),
        P(),
    )
    out_specs = (
        P("ctx", "head", None),
        P("ctx", "head"),
        P(("ctx", "head"), None),
        P(("ctx", "head"), None),
    )
    return jax.shard_map(
        per_device, mesh=mesh, in_specs=in_specs, out_specs=out_specs, check_vma=False
    )
```

```python
import functools

import jax
import jax.numpy as jnp
from jax import lax
from jax.experimental import pallas as pl
from jax.experimental.pallas import tpu as pltpu
from jax.sharding import PartitionSpec as P

SPAN = 4
LAT = 512
ROPE = 64
WIDE = 640
SCALE = 192.0 ** (-0.5)
SCALE_LOG2 = SCALE * 1.4426950408889634
CHUNK = 256
SPLITS = ((256, 384), (0, 256))

NT = (((1,), (1,)), ((), ()))
TN = (((0,), (0,)), ((), ()))


def dot(a, b, dims=(((1,), (0,)), ((), ()))):
    return lax.dot_general(a, b, dims, preferred_element_type=jnp.float32)


def kernel(
    n_ctx, heads,
    pos_hbm, kv_hbm, kr_hbm, qr_hbm, q_hbm, g_hbm,
    dq_ref, dqr_ref, dkv_ref, dkr_ref,
    block_pos, kv_ref, kr_ref, qr_ref, kvr, qv, gv, rot32, s_a, s_b, dp_a, dp_b, ds_t, w_t,
    d0, d1, as0, as1, ar0, ar1, bs0, bs1, br0, br1, cs0, cs1, cr0, cr1,
    in_sem, f_send, f_recv, p_send, p_recv,
    a_send, a_recv, b_send, b_recv, c_send, c_recv,
):
    c = lax.axis_index("ctx")
    h = lax.axis_index("head")
    z = lax.div(h, 2)
    a = lax.rem(h, 2)
    sib = z * 2 + (1 - a)
    zpart = (1 - z) * 2 + a
    rows = qv.shape[0]
    half = rows // 2

    def ctx_at(k):
        return lax.rem(c + k + n_ctx, n_ctx)

    load_keys = [
        pltpu.make_async_copy(kv_hbm, kv_ref, in_sem.at[0]),
        pltpu.make_async_copy(kr_hbm, kr_ref, in_sem.at[1]),
    ]
    load_rot = pltpu.make_async_copy(qr_hbm, qr_ref, in_sem.at[2])
    loads = [
        pltpu.make_async_copy(pos_hbm, block_pos, in_sem.at[3]),
        pltpu.make_async_copy(q_hbm, qv.at[:, pl.ds(0, LAT)], in_sem.at[4]),
        pltpu.make_async_copy(g_hbm, gv, in_sem.at[5]),
    ]
    for load in [*load_keys, load_rot, *loads]:
        load.start()

    barrier = pltpu.get_barrier_semaphore()
    peers = [(ctx_at(k), h) for k in (1, 2, 3, -1, -2, -3)] + [(c, sib), (c, zpart)]
    for peer in peers:
        pl.semaphore_signal(barrier, inc=1, device_id=peer, device_id_type=pl.DeviceIdType.MESH)

    for load in load_keys:
        load.wait()
    kvr[0, :, :, pl.ds(0, LAT)] = kv_ref[...].reshape(2, 64, LAT)
    rot = kr_ref[...].astype(jnp.float32)
    kvr[0, :, :, pl.ds(LAT, 128)] = jnp.concatenate(
        [rot, jnp.zeros_like(rot)], axis=0
    ).T.astype(jnp.bfloat16).reshape(2, 64, 128)

    pl.semaphore_wait(barrier, len(peers))

    def remote(src, dst, send, recv, peer):
        return pltpu.make_async_remote_copy(
            src_ref=src, dst_ref=dst, send_sem=send, recv_sem=recv,
            device_id=peer, device_id_type=pl.DeviceIdType.MESH,
        )

    forward = {}
    for k in (2, 1, 3):
        forward[k] = remote(
            kvr.at[0, a], kvr.at[k, a], f_send.at[k - 1], f_recv.at[k - 1], (ctx_at(k), h)
        )
        forward[k].start()

    load_rot.wait()
    tokens = qr_ref.shape[0]
    low = lax.broadcasted_iota(jnp.int32, (tokens, 128), 1) < ROPE
    for j in range(heads // 2):
        tile = qr_ref[:, pl.ds(j * 128, 128)].astype(jnp.float32)
        rot32[pl.ds(2 * j, tokens, stride=heads), :] = jnp.where(low, tile, 0.0)
        rot32[pl.ds(2 * j + 1, tokens, stride=heads), :] = jnp.where(
            low, pltpu.roll(tile, 64, 1), 0.0
        )
    qv[:, pl.ds(LAT, 128)] = rot32[...].astype(jnp.bfloat16)

    passed = {}
    for k in (1, 3, 2):
        forward[k].wait_recv()
        passed[k] = remote(
            kvr.at[k, a], kvr.at[k, a], p_send.at[k - 1], p_recv.at[k - 1], (c, sib)
        )
        passed[k].start()
    for load in loads:
        load.wait()
    for k in (1, 3, 2):
        passed[k].wait_recv()

    key_pos = [
        block_pos[2 * ctx_at(-(slot // 2)) + slot % 2] for slot in range(2 * SPAN)
    ]
    query_pos = [block_pos[2 * c], block_pos[2 * c + 1]]

    def score(start, s_buf, dp_buf):
        at = pl.ds(start, CHUNK)
        keys = kvr[...].reshape(SPAN * 128, WIDE)
        s_buf[...] = dot(keys, qv[at, :], NT)
        dp_buf[...] = dot(keys[:, :LAT], gv[at, :], NT)

    lane_row = lax.broadcasted_iota(jnp.int32, (64, CHUNK), 1)
    sub_row = lax.broadcasted_iota(jnp.int32, (64, CHUNK), 0)

    def soften(start, s_buf, dp_buf):
        at = pl.ds(start, CHUNK)
        second = start // half
        pos = query_pos[second] * 64
        ahead = lax.div(lane_row + (start - second * half), heads) - sub_row
        top = None
        for slot in range(2 * SPAN):
            part = pl.ds(slot * 64, 64)
            seen = ahead >= key_pos[slot] * 64 - pos
            s = jnp.where(seen, s_buf[part, :], -jnp.inf)
            s_buf[part, :] = s
            m = jnp.max(s, axis=0, keepdims=True)
            top = m if top is None else jnp.maximum(top, m)
        total = None
        for slot in range(2 * SPAN):
            part = pl.ds(slot * 64, 64)
            e = jnp.exp2((s_buf[part, :] - top) * SCALE_LOG2)
            s_buf[part, :] = e
            t = jnp.sum(e, axis=0, keepdims=True)
            total = t if total is None else total + t
        inv = 1.0 / total
        delta = None
        for slot in range(2 * SPAN):
            part = pl.ds(slot * 64, 64)
            w = (s_buf[part, :] * inv).astype(jnp.bfloat16)
            w_t[part, at] = w
            t = jnp.sum(w.astype(jnp.float32) * dp_buf[part, :], axis=0, keepdims=True)
            delta = t if delta is None else delta + t
        for slot in range(2 * SPAN):
            part = pl.ds(slot * 64, 64)
            ds_t[part, at] = (
                (s_buf[part, :] * inv) * (dp_buf[part, :] - delta)
            ).astype(jnp.bfloat16)

    score(0, s_a, dp_a)

    for start in range(0, rows, 2 * CHUNK):
        score(start + CHUNK, s_b, dp_b)
        soften(start, s_a, dp_a)
        if start + 2 * CHUNK < rows:
            score(start + 2 * CHUNK, s_a, dp_a)
        soften(start + CHUNK, s_b, dp_b)

    d, asb, arb, bsb, brb = (d0, d1), (as0, as1), (ar0, ar1), (bs0, bs1), (br0, br1)
    csb, crb = (cs0, cs1), (cr0, cr1)

    def key_grads(n):
        first, width = SPLITS[n]
        shape = (2 * SPAN, 2, 32, width)
        part = SCALE * dot(ds_t[...], qv[:, pl.ds(first, width)])
        latent = min(width, LAT - first)
        other = dot(w_t[...], gv[:, pl.ds(first, latent)])
        if latent == width:
            d[n][...] = (part + other).reshape(shape)
        else:
            d[n][:, :, :, pl.ds(0, latent)] = (part[:, :latent] + other).reshape(shape[:3] + (latent,))
            d[n][:, :, :, pl.ds(latent, width - latent)] = part[:, latent:].reshape(
                shape[:3] + (width - latent,)
            )
        asb[n][...] = d[n][:, pl.ds(1 - a, 1)].reshape(2 * SPAN, 32, width).astype(jnp.bfloat16)
        copy = remote(asb[n], arb[n], a_send.at[n], a_recv.at[n], (c, sib))
        copy.start()
        return copy

    def own(n, k):
        width = SPLITS[n][1]
        return d[n][pl.ds(2 * k, 2), pl.ds(a, 1)].reshape(2, 32, width)

    def add_cores(n, copy):
        copy.wait_recv()
        sends = []
        for k in (2, 1, 3):
            got = arb[n][pl.ds(2 * k, 2)].astype(jnp.float32)
            bsb[n][k - 1] = (own(n, k) + got).astype(jnp.bfloat16)
            sends.append(remote(
                bsb[n].at[k - 1], brb[n].at[k - 1], b_send.at[n, k - 1], b_recv.at[n, k - 1],
                (ctx_at(-k), h),
            ))
            sends[-1].start()
        return sends

    def add_context(n, sends):
        for copy in sends:
            copy.wait_recv()
        sums = own(n, 0) + arb[n][pl.ds(0, 2)].astype(jnp.float32)
        for k in (1, 2, 3):
            sums = sums + brb[n][k - 1].astype(jnp.float32)
        width = SPLITS[n][1]
        d[n][pl.ds(0, 2), pl.ds(a, 1)] = sums.reshape(2, 1, 32, width)
        csb[n][...] = d[n][pl.ds(1 - z, 1), pl.ds(a, 1)].reshape(32, width).astype(jnp.bfloat16)
        copy = remote(csb[n], crb[n], c_send.at[n], c_recv.at[n], (c, zpart))
        copy.start()
        return copy

    def finish(n, copy):
        copy.wait_recv()
        first, width = SPLITS[n]
        result = d[n][pl.ds(z, 1), pl.ds(a, 1)].reshape(32, width) + crb[n][...].astype(jnp.float32)
        result = result.astype(jnp.bfloat16)
        latent = min(width, LAT - first)
        dkv_ref[:, pl.ds(first, latent)] = result[:, :latent]
        if latent < width:
            dkr_ref[...] = result[:, latent:latent + ROPE]

    def query_grads(i):
        start = i * CHUNK
        at = pl.ds(start, CHUNK)
        keys = kvr[...].reshape(SPAN * 128, WIDE)
        grad = SCALE * dot(ds_t[:, at], keys, TN)
        dq_ref[at, :] = grad[:, :LAT].astype(jnp.bfloat16)
        rot32[at, :] = grad[:, LAT:]

    a0 = key_grads(0)
    a1 = key_grads(1)
    b0 = add_cores(0, a0)
    query_grads(0)
    query_grads(1)
    b1 = add_cores(1, a1)
    query_grads(2)
    query_grads(3)
    query_grads(4)
    c0 = add_context(0, b0)
    query_grads(5)
    query_grads(6)
    query_grads(7)

    for j in range(heads // 2):
        even = rot32[pl.ds(2 * j, tokens, stride=heads), :]
        odd = rot32[pl.ds(2 * j + 1, tokens, stride=heads), :]
        dqr_ref[:, pl.ds(j * 128, 128)] = jnp.where(
            low, even, pltpu.roll(odd, 64, 1)
        ).astype(jnp.bfloat16)

    c1 = add_context(1, b1)
    finish(0, c0)
    for copy in [*forward.values(), *passed.values(), a0, a1, *b0, *b1, c0]:
        copy.wait_send()
    finish(1, c1)
    c1.wait_send()


def move(*refs):
    sources, targets, sem = refs[:4], refs[4:8], refs[8]
    copies = [
        pltpu.make_async_copy(s, t, sem.at[i]) for i, (s, t) in enumerate(zip(sources, targets))
    ]
    for copy in copies:
        copy.start()
    for copy in copies:
        copy.wait()


def per_device(q_latent, q_rope, kv_latent, k_rope, out_grad, block_pos):
    tokens, heads, lat = q_latent.shape
    rows = tokens * heads
    keys = SPAN * tokens
    n_ctx = lax.axis_size("ctx")
    bf16, f32 = jnp.bfloat16, jnp.float32
    vmem = pl.BlockSpec(memory_space=pltpu.VMEM)
    hbm = pl.BlockSpec(memory_space=pltpu.HBM)
    widths = [width for _, width in SPLITS]

    def pairs(shape, kind):
        return [pltpu.VMEM(shape + (width,), kind) for width in widths]

    dma = pltpu.SemaphoreType.DMA
    scratch = [
        pltpu.SMEM(block_pos.shape, jnp.int32),
        pltpu.VMEM((tokens, lat), bf16),
        pltpu.VMEM((ROPE, tokens), bf16),
        pltpu.VMEM((tokens, heads * ROPE), bf16),
        pltpu.VMEM((SPAN, 2, 64, WIDE), bf16),
        pltpu.VMEM((rows, WIDE), bf16),
        pltpu.VMEM((rows, lat), bf16),
        pltpu.VMEM((rows, 128), f32),
        *[pltpu.VMEM((keys, CHUNK), f32) for _ in range(4)],
        pltpu.VMEM((keys, rows), bf16),
        pltpu.VMEM((keys, rows), bf16),
        *pairs((2 * SPAN, 2, 32), f32),
        *pairs((2 * SPAN, 32), bf16),
        *pairs((2 * SPAN, 32), bf16),
        *pairs((3, 2, 32), bf16),
        *pairs((3, 2, 32), bf16),
        *pairs((32,), bf16),
        *pairs((32,), bf16),
        dma((6,)),
        dma((3,)), dma((3,)), dma((3,)), dma((3,)),
        dma((2,)), dma((2,)), dma((2, 3)), dma((2, 3)), dma((2,)), dma((2,)),
    ]
    macs = rows * keys * (WIDE * 3 + 2 * lat)
    dq, dqr, dkv, dkr = pl.pallas_call(
        functools.partial(kernel, n_ctx, heads),
        out_shape=(
            pltpu.VMEM((rows, lat), bf16),
            pltpu.VMEM((tokens, heads * ROPE), bf16),
            pltpu.VMEM((tokens // 4, lat), bf16),
            pltpu.VMEM((tokens // 4, ROPE), bf16),
        ),
        in_specs=[hbm] * 6,
        out_specs=(vmem,) * 4,
        scratch_shapes=scratch,
        compiler_params=pltpu.CompilerParams(
            collective_id=0, has_side_effects=True, vmem_limit_bytes=56 * 2**20
        ),
        cost_estimate=pl.CostEstimate(
            flops=2 * macs, bytes_accessed=7 * 2**20, transcendentals=rows * keys
        ),
    )(
        block_pos, kv_latent, k_rope.T, q_rope,
        q_latent.reshape(rows, lat), out_grad.reshape(rows, lat),
    )
    results = (dq, dqr, dkv, dkr)
    dq, dqr, dkv, dkr = pl.pallas_call(
        move,
        out_shape=tuple(jax.ShapeDtypeStruct(r.shape, r.dtype) for r in results),
        in_specs=[vmem] * 4,
        out_specs=(hbm,) * 4,
        scratch_shapes=[dma((4,))],
    )(*results)
    return dq.reshape(tokens, heads, lat), dqr, dkv, dkr


def solution(mesh):
    in_specs = (
        P("ctx", "head", None),
        P("ctx", "head"),
        P("ctx", None),
        P("ctx", None),
        P("ctx", "head", None),
        P(),
    )
    out_specs = (
        P("ctx", "head", None),
        P("ctx", "head"),
        P(("ctx", "head"), None),
        P(("ctx", "head"), None),
    )
    return jax.shard_map(
        per_device, mesh=mesh, in_specs=in_specs, out_specs=out_specs, check_vma=False
    )
```

```python
import functools

import jax
import jax.numpy as jnp
from jax import lax
from jax.experimental import pallas as pl
from jax.experimental.pallas import tpu as pltpu
from jax.sharding import PartitionSpec as P

SPAN = 4
LAT = 512
ROPE = 64
WIDE = 640
SCALE = 192.0 ** (-0.5)
SCALE_LOG2 = SCALE * 1.4426950408889634
CHUNK = 256
ORDER = (0, 1, 3, 2)
PLACE = tuple(ORDER.index(k) for k in range(SPAN))
GROUPS = ((0, 1), (1, 2), (3, 1))
SPLITS = ((0, 256), (256, 256), (512, 128))

NT = (((1,), (1,)), ((), ()))
TN = (((0,), (0,)), ((), ()))


def dot(a, b, dims=(((1,), (0,)), ((), ()))):
    return lax.dot_general(a, b, dims, preferred_element_type=jnp.float32)


def kernel(
    n_ctx, heads,
    pos_hbm, kv_hbm, kr_hbm, qr_hbm, q_hbm, g_hbm,
    dq_ref, dqr_ref, dkv_ref, dkr_ref,
    block_pos, kv_ref, kr_ref, qr_ref, kvr, qv, gv, rot32, s_a, s_b, e_buf, dp_buf, tops, sums, ds_t, w_t,
    *rest,
):
    parts = len(SPLITS)
    d, asb, arb, ysb, yrb, bsb, brb, csb, crb = [
        rest[i * parts:(i + 1) * parts] for i in range(9)
    ]
    (
        in_sem, f_send, f_recv, p_send, p_recv,
        a_send, a_recv, y_send, y_recv, b_send, b_recv, c_send, c_recv,
    ) = rest[9 * parts:]
    c = lax.axis_index("ctx")
    h = lax.axis_index("head")
    z = lax.div(h, 2)
    a = lax.rem(h, 2)
    sib = z * 2 + (1 - a)
    zpart = (1 - z) * 2 + a
    rows = qv.shape[0]
    half = rows // 2
    s_bufs = (s_a, s_b)

    def ctx_at(k):
        return lax.rem(c + k + n_ctx, n_ctx)

    load_keys = [
        pltpu.make_async_copy(kv_hbm, kv_ref, in_sem.at[0]),
        pltpu.make_async_copy(kr_hbm, kr_ref, in_sem.at[1]),
    ]
    load_rot = pltpu.make_async_copy(qr_hbm, qr_ref, in_sem.at[2])
    loads = [
        pltpu.make_async_copy(pos_hbm, block_pos, in_sem.at[3]),
        pltpu.make_async_copy(q_hbm, qv.at[:, pl.ds(0, LAT)], in_sem.at[4]),
        pltpu.make_async_copy(g_hbm, gv, in_sem.at[5]),
    ]
    for load in load_keys:
        load.start()

    barrier = pltpu.get_barrier_semaphore()
    peers = [(ctx_at(k), h) for k in (1, 3, -1, -3)] + [(c, sib), (c, zpart)]
    for peer in peers:
        pl.semaphore_signal(barrier, inc=1, device_id=peer, device_id_type=pl.DeviceIdType.MESH)

    for load in [load_rot, *loads]:
        load.start()

    for load in load_keys:
        load.wait()
    kvr[0, :, :, :, pl.ds(0, LAT)] = kv_ref[...].reshape(2, 2, 32, LAT)
    rot = kr_ref[...].astype(jnp.float32)
    kvr[0, :, :, :, pl.ds(LAT, 128)] = jnp.concatenate(
        [rot, jnp.zeros_like(rot)], axis=0
    ).T.astype(jnp.bfloat16).reshape(2, 2, 32, 128)

    pl.semaphore_wait(barrier, len(peers))

    def remote(src, dst, send, recv, peer):
        return pltpu.make_async_remote_copy(
            src_ref=src, dst_ref=dst, send_sem=send, recv_sem=recv,
            device_id=peer, device_id_type=pl.DeviceIdType.MESH,
        )

    flights = []
    arrived = {}

    def key_copy(index, source, target, peer):
        copy = remote(kvr.at[source], kvr.at[target], f_send.at[index], f_recv.at[index], peer)
        copy.start()
        flights.append(copy)
        return copy

    for index, (k, piece) in enumerate(((1, 0), (3, 1), (1, 1), (3, 0))):
        arrived[k, piece] = key_copy(
            index, (0, a, piece), (PLACE[k], a, piece), (ctx_at(k), h)
        )

    def relay():
        arrived[1, 0].wait_recv()
        arrived[2, 0] = key_copy(4, (PLACE[1], a, 0), (PLACE[2], a, 0), (ctx_at(1), h))
        arrived[3, 1].wait_recv()
        arrived[2, 1] = key_copy(5, (PLACE[3], a, 1), (PLACE[2], a, 1), (ctx_at(-1), h))

    load_rot.wait()
    tokens = qr_ref.shape[0]
    low = lax.broadcasted_iota(jnp.int32, (tokens, 128), 1) < ROPE
    for j in range(heads // 2):
        tile = qr_ref[:, pl.ds(j * 128, 128)].astype(jnp.float32)
        rot32[pl.ds(2 * j, tokens, stride=heads), :] = jnp.where(low, tile, 0.0)
        rot32[pl.ds(2 * j + 1, tokens, stride=heads), :] = jnp.where(
            low, pltpu.roll(tile, 64, 1), 0.0
        )
    qv[:, pl.ds(LAT, 128)] = rot32[...].astype(jnp.bfloat16)

    for load in loads:
        load.wait()
    passed = {}

    def pass_on(k):
        for piece in (0, 1):
            if (k, piece) not in ((1, 0), (3, 1)):
                arrived[k, piece].wait_recv()
        passed[k] = remote(
            kvr.at[PLACE[k], a], kvr.at[PLACE[k], a], p_send.at[k - 1], p_recv.at[k - 1], (c, sib)
        )
        passed[k].start()

    key_pos = [
        block_pos[2 * ctx_at(-ORDER[slot // 2]) + slot % 2] for slot in range(2 * SPAN)
    ]
    query_pos = [block_pos[2 * c], block_pos[2 * c + 1]]
    lane_row = lax.broadcasted_iota(jnp.int32, (64, CHUNK), 1)
    sub_row = lax.broadcasted_iota(jnp.int32, (64, CHUNK), 0)
    chunks = rows // CHUNK

    def score(group, i):
        first, count = GROUPS[group]
        at = pl.ds(i * CHUNK, CHUNK)
        keys = kvr[pl.ds(first, count)].reshape(count * 128, WIDE)
        s_buf = s_bufs[i % 2]
        s_buf[pl.ds(0, count * 128), :] = dot(keys, qv[at, :], NT)
        dp_buf[pl.ds(first * 128, count * 128), at] = dot(keys[:, :LAT], gv[at, :], NT)

    def soften(group, i):
        first, count = GROUPS[group]
        at = pl.ds(i * CHUNK, CHUNK)
        s_buf = s_bufs[i % 2]
        second = i * CHUNK // half
        ahead = lax.div(lane_row + (i * CHUNK - second * half), heads) - sub_row
        top = jnp.full((1, CHUNK), -1e30, jnp.float32)
        for j in range(2 * count):
            part = pl.ds(j * 64, 64)
            seen = ahead >= (key_pos[2 * first + j] - query_pos[second]) * 64
            s = jnp.where(seen, s_buf[part, :], -jnp.inf)
            s_buf[part, :] = s
            top = jnp.maximum(top, jnp.max(s, axis=0, keepdims=True))
        total = jnp.zeros((1, CHUNK), jnp.float32)
        for j in range(2 * count):
            e = jnp.exp2((s_buf[pl.ds(j * 64, 64), :] - top) * SCALE_LOG2)
            e_buf[pl.ds(first * 128 + j * 64, 64), at] = e
            total = total + jnp.sum(e, axis=0, keepdims=True)
        tops[pl.ds(group, 1), at] = top
        sums[pl.ds(group, 1), at] = total

    def join(i):
        at = pl.ds(i * CHUNK, CHUNK)
        parts = range(len(GROUPS))
        top_of = [tops[pl.ds(g, 1), at] for g in parts]
        top = functools.reduce(jnp.maximum, top_of)
        part_of = [jnp.exp2((t - top) * SCALE_LOG2) for t in top_of]
        total = sum(f * sums[pl.ds(g, 1), at] for g, f in zip(parts, part_of))
        inv = 1.0 / total
        factor = []
        for g in parts:
            factor += [part_of[g] * inv] * (2 * GROUPS[g][1])
        delta = jnp.zeros((1, CHUNK), jnp.float32)
        for slot in range(2 * SPAN):
            part = pl.ds(slot * 64, 64)
            w = (e_buf[part, at] * factor[slot]).astype(jnp.bfloat16)
            w_t[part, at] = w
            delta = delta + jnp.sum(
                w.astype(jnp.float32) * dp_buf[part, at], axis=0, keepdims=True
            )
        for slot in range(2 * SPAN):
            part = pl.ds(slot * 64, 64)
            ds_t[part, at] = (
                (e_buf[part, at] * factor[slot]) * (dp_buf[part, at] - delta)
            ).astype(jnp.bfloat16)

    score(0, 0)
    for i in range(chunks):
        if i == 2:
            relay()
        if i == 5:
            pass_on(1)
            pass_on(3)
        if i + 1 < chunks:
            score(0, i + 1)
        soften(0, i)
    passed[1].wait_recv()
    passed[3].wait_recv()
    score(1, 0)
    for i in range(chunks):
        if i == 4:
            pass_on(2)
        if i + 1 < chunks:
            score(1, i + 1)
        soften(1, i)
    passed[2].wait_recv()
    score(2, 0)
    for i in range(chunks):
        if i + 1 < chunks:
            score(2, i + 1)
        soften(2, i)
        join(i)


    def key_grads(n):
        first, width = SPLITS[n]
        part = SCALE * dot(ds_t[...], qv[:, pl.ds(first, width)])
        if first < LAT:
            part = part + dot(w_t[...], gv[:, pl.ds(first, width)])
        d[n][...] = part.reshape(2 * SPAN, 2, 32, width)
        asb[n][...] = d[n][:, pl.ds(1 - a, 1)].reshape(2 * SPAN, 32, width).astype(jnp.bfloat16)
        copy = remote(asb[n], arb[n], a_send.at[n], a_recv.at[n], (c, sib))
        copy.start()
        flights.append(copy)
        return copy

    def own(n, k, piece=None):
        width = SPLITS[n][1]
        if piece is None:
            return d[n][pl.ds(2 * PLACE[k], 2), pl.ds(a, 1)].reshape(2, 32, width)
        return d[n][pl.ds(2 * PLACE[k] + piece, 1), pl.ds(a, 1)].reshape(32, width)

    def sum_to(n, k, piece):
        index = k - 1 + piece
        copy = remote(
            bsb[n].at[index], brb[n].at[index], b_send.at[n, index], b_recv.at[n, index],
            (ctx_at(-k), h),
        )
        copy.start()
        flights.append(copy)
        return copy

    def add_cores(n, copy):
        copy.wait_recv()
        width = SPLITS[n][1]
        for k in (2, 1, 3, 0):
            got = arb[n][pl.ds(2 * PLACE[k], 2)].astype(jnp.float32)
            added = own(n, k) + got
            if k == 2:
                ysb[n][...] = added.astype(jnp.bfloat16)
                onward = []
                for piece, step in ((0, -1), (1, 1)):
                    onward.append(remote(
                        ysb[n].at[piece], yrb[n].at[piece], y_send.at[n, piece],
                        y_recv.at[n, piece], (ctx_at(step), h),
                    ))
                    onward[-1].start()
                    flights.append(onward[-1])
            else:
                d[n][pl.ds(2 * PLACE[k], 2), pl.ds(a, 1)] = added.reshape(2, 1, 32, width)
            if k == 1:
                bsb[n][1] = added[1].astype(jnp.bfloat16)
                sent = [sum_to(n, 1, 1)]
            if k == 3:
                bsb[n][2] = added[0].astype(jnp.bfloat16)
                sent.append(sum_to(n, 3, 0))
        return onward, sent

    def merge(n, onward, sent):
        for copy, (k, piece) in zip(onward, ((1, 0), (3, 1))):
            copy.wait_recv()
            added = own(n, k, piece) + yrb[n][piece].astype(jnp.float32)
            bsb[n][k - 1 + piece] = added.astype(jnp.bfloat16)
            sent.append(sum_to(n, k, piece))
        return sent

    def add_context(n, sent):
        for copy in sent:
            copy.wait_recv()
        width = SPLITS[n][1]
        near = brb[n][pl.ds(0, 2)].astype(jnp.float32)
        far = brb[n][pl.ds(2, 2)].astype(jnp.float32)
        d[n][pl.ds(0, 2), pl.ds(a, 1)] = (own(n, 0) + near + far).reshape(2, 1, 32, width)
        csb[n][...] = d[n][pl.ds(1 - z, 1), pl.ds(a, 1)].reshape(32, width).astype(jnp.bfloat16)
        copy = remote(csb[n], crb[n], c_send.at[n], c_recv.at[n], (c, zpart))
        copy.start()
        flights.append(copy)
        return copy

    def finish(n, copy):
        copy.wait_recv()
        first, width = SPLITS[n]
        result = d[n][pl.ds(z, 1), pl.ds(a, 1)].reshape(32, width) + crb[n][...].astype(jnp.float32)
        result = result.astype(jnp.bfloat16)
        if first < LAT:
            dkv_ref[:, pl.ds(first, width)] = result
        else:
            dkr_ref[...] = result[:, :ROPE]

    def query_grads(i):
        start = i * CHUNK
        at = pl.ds(start, CHUNK)
        keys = kvr[...].reshape(SPAN * 128, WIDE)
        grad = SCALE * dot(ds_t[:, at], keys, TN)
        dq_ref[at, :] = grad[:, :LAT].astype(jnp.bfloat16)
        rot32[at, :] = grad[:, LAT:]

    a0 = key_grads(0)
    a1 = key_grads(1)
    y0 = add_cores(0, a0)
    a2 = key_grads(2)
    query_grads(0)
    y1 = add_cores(1, a1)
    query_grads(1)
    b0 = merge(0, *y0)
    y2 = add_cores(2, a2)
    query_grads(2)
    b1 = merge(1, *y1)
    query_grads(3)
    c0 = add_context(0, b0)
    b2 = merge(2, *y2)
    query_grads(4)
    c1 = add_context(1, b1)
    query_grads(5)
    query_grads(6)
    query_grads(7)

    for j in range(heads // 2):
        even = rot32[pl.ds(2 * j, tokens, stride=heads), :]
        odd = rot32[pl.ds(2 * j + 1, tokens, stride=heads), :]
        dqr_ref[:, pl.ds(j * 128, 128)] = jnp.where(
            low, even, pltpu.roll(odd, 64, 1)
        ).astype(jnp.bfloat16)

    c2 = add_context(2, b2)
    finish(0, c0)
    finish(1, c1)
    for copy in [*passed.values(), *flights]:
        copy.wait_send()
    finish(2, c2)


def move(*refs):
    sources, targets, sem = refs[:4], refs[4:8], refs[8]
    copies = [
        pltpu.make_async_copy(s, t, sem.at[i]) for i, (s, t) in enumerate(zip(sources, targets))
    ]
    for copy in copies:
        copy.start()
    for copy in copies:
        copy.wait()


def per_device(q_latent, q_rope, kv_latent, k_rope, out_grad, block_pos):
    tokens, heads, lat = q_latent.shape
    rows = tokens * heads
    keys = SPAN * tokens
    n_ctx = lax.axis_size("ctx")
    bf16, f32 = jnp.bfloat16, jnp.float32
    vmem = pl.BlockSpec(memory_space=pltpu.VMEM)
    hbm = pl.BlockSpec(memory_space=pltpu.HBM)
    widths = [width for _, width in SPLITS]
    n = len(SPLITS)

    def pairs(shape, kind):
        return [pltpu.VMEM(shape + (width,), kind) for width in widths]

    dma = pltpu.SemaphoreType.DMA
    scratch = [
        pltpu.SMEM(block_pos.shape, jnp.int32),
        pltpu.VMEM((tokens, lat), bf16),
        pltpu.VMEM((ROPE, tokens), bf16),
        pltpu.VMEM((tokens, heads * ROPE), bf16),
        pltpu.VMEM((SPAN, 2, 2, 32, WIDE), bf16),
        pltpu.VMEM((rows, WIDE), bf16),
        pltpu.VMEM((rows, lat), bf16),
        pltpu.VMEM((rows, 128), f32),
        *[pltpu.VMEM((keys // 2, CHUNK), f32) for _ in range(2)],
        *[pltpu.VMEM((keys, rows), f32) for _ in range(2)],
        *[pltpu.VMEM((8, rows), f32) for _ in range(2)],
        pltpu.VMEM((keys, rows), bf16),
        pltpu.VMEM((keys, rows), bf16),
        *pairs((2 * SPAN, 2, 32), f32),
        *pairs((2 * SPAN, 32), bf16),
        *pairs((2 * SPAN, 32), bf16),
        *pairs((2, 32), bf16),
        *pairs((2, 32), bf16),
        *pairs((4, 32), bf16),
        *pairs((4, 32), bf16),
        *pairs((32,), bf16),
        *pairs((32,), bf16),
        dma((6,)), dma((6,)), dma((6,)), dma((3,)), dma((3,)),
        dma((n,)), dma((n,)), dma((n, 2)), dma((n, 2)), dma((n, 4)), dma((n, 4)),
        dma((n,)), dma((n,)),
    ]
    macs = rows * keys * (WIDE * 3 + 2 * lat)
    dq, dqr, dkv, dkr = pl.pallas_call(
        functools.partial(kernel, n_ctx, heads),
        out_shape=(
            pltpu.VMEM((rows, lat), bf16),
            pltpu.VMEM((tokens, heads * ROPE), bf16),
            pltpu.VMEM((tokens // 4, lat), bf16),
            pltpu.VMEM((tokens // 4, ROPE), bf16),
        ),
        in_specs=[hbm] * 6,
        out_specs=(vmem,) * 4,
        scratch_shapes=scratch,
        compiler_params=pltpu.CompilerParams(
            collective_id=0, has_side_effects=True, vmem_limit_bytes=56 * 2**20
        ),
        cost_estimate=pl.CostEstimate(
            flops=2 * macs, bytes_accessed=7 * 2**20, transcendentals=rows * keys
        ),
    )(
        block_pos, kv_latent, k_rope.T, q_rope,
        q_latent.reshape(rows, lat), out_grad.reshape(rows, lat),
    )
    results = (dq, dqr, dkv, dkr)
    dq, dqr, dkv, dkr = pl.pallas_call(
        move,
        out_shape=tuple(jax.ShapeDtypeStruct(r.shape, r.dtype) for r in results),
        in_specs=[vmem] * 4,
        out_specs=(hbm,) * 4,
        scratch_shapes=[dma((4,))],
        compiler_params=pltpu.CompilerParams(vmem_limit_bytes=2**20),
    )(*results)
    return dq.reshape(tokens, heads, lat), dqr, dkv, dkr


def solution(mesh):
    in_specs = (
        P("ctx", "head", None),
        P("ctx", "head"),
        P("ctx", None),
        P("ctx", None),
        P("ctx", "head", None),
        P(),
    )
    out_specs = (
        P("ctx", "head", None),
        P("ctx", "head"),
        P(("ctx", "head"), None),
        P(("ctx", "head"), None),
    )
    return jax.shard_map(
        per_device, mesh=mesh, in_specs=in_specs, out_specs=out_specs, check_vma=False
    )
```

```python
import functools

import jax
import jax.numpy as jnp
from jax import lax
from jax.experimental import pallas as pl
from jax.experimental.pallas import tpu as pltpu
from jax.sharding import PartitionSpec as P

SPAN = 4
LAT = 512
ROPE = 64
WIDE = 640
SCALE = 192.0 ** (-0.5)
SCALE_LOG2 = SCALE * 1.4426950408889634
CHUNK = 256
ORDER = (0, 1, 3, 2)
PLACE = tuple(ORDER.index(k) for k in range(SPAN))
GROUPS = ((0, 1), (1, 2), (3, 1))
SPLITS = ((256, 384), (0, 256))

PIECES = 8

NT = (((1,), (1,)), ((), ()))
TN = (((0,), (0,)), ((), ()))


def dot(a, b, dims=(((1,), (0,)), ((), ()))):
    return lax.dot_general(a, b, dims, preferred_element_type=jnp.float32)


def kernel(
    n_ctx, heads,
    pos_hbm, kv_hbm, kr_hbm, qr_hbm, q_hbm, g_hbm,
    dq_ref, dqr_ref, dkv_ref, dkr_ref,
    block_pos, kv_ref, kr_ref, qr_ref, kvr, qv, gv, rot32, s_a, s_b, e_buf, dp_buf, tops, sums, ds_t, w_t,
    d0, d1, as0, as1, ar0, ar1, bs0, bs1, br0, br1, cs0, cs1, cr0, cr1,
    in_sem, f_send, f_recv, p_send, p_recv,
    a_send, a_recv, b_send, b_recv, c_send, c_recv,
):
    c = lax.axis_index("ctx")
    h = lax.axis_index("head")
    z = lax.div(h, 2)
    a = lax.rem(h, 2)
    sib = z * 2 + (1 - a)
    zpart = (1 - z) * 2 + a
    rows = qv.shape[0]
    half = rows // 2
    s_bufs = (s_a, s_b)

    def ctx_at(k):
        return lax.rem(c + k + n_ctx, n_ctx)

    load_keys = [
        pltpu.make_async_copy(kv_hbm, kv_ref, in_sem.at[0]),
        pltpu.make_async_copy(kr_hbm, kr_ref, in_sem.at[1]),
    ]
    load_rot = pltpu.make_async_copy(qr_hbm, qr_ref, in_sem.at[2])
    loads = [
        pltpu.make_async_copy(pos_hbm, block_pos, in_sem.at[3]),
        pltpu.make_async_copy(q_hbm, qv.at[:, pl.ds(0, LAT)], in_sem.at[4]),
        pltpu.make_async_copy(g_hbm, gv, in_sem.at[5]),
    ]
    for load in load_keys:
        load.start()

    barrier = pltpu.get_barrier_semaphore()
    peers = [(ctx_at(k), h) for k in (1, 2, 3, -1, -2, -3)] + [(c, sib), (c, zpart)]
    for peer in peers:
        pl.semaphore_signal(barrier, inc=1, device_id=peer, device_id_type=pl.DeviceIdType.MESH)

    for load in [load_rot, *loads]:
        load.start()

    for load in load_keys:
        load.wait()
    kvr[0, :, :, pl.ds(0, LAT)] = kv_ref[...].reshape(2, 64, LAT)
    rot = kr_ref[...].astype(jnp.float32)
    kvr[0, :, :, pl.ds(LAT, 128)] = jnp.concatenate(
        [rot, jnp.zeros_like(rot)], axis=0
    ).T.astype(jnp.bfloat16).reshape(2, 64, 128)

    pl.semaphore_wait(barrier, len(peers))

    def remote(src, dst, send, recv, peer):
        return pltpu.make_async_remote_copy(
            src_ref=src, dst_ref=dst, send_sem=send, recv_sem=recv,
            device_id=peer, device_id_type=pl.DeviceIdType.MESH,
        )

    forward = {}
    for k in (1, 3, 2):
        forward[k] = remote(
            kvr.at[0, a], kvr.at[PLACE[k], a], f_send.at[k - 1], f_recv.at[k - 1], (ctx_at(k), h)
        )
        forward[k].start()

    load_rot.wait()
    tokens = qr_ref.shape[0]
    low = lax.broadcasted_iota(jnp.int32, (tokens, 128), 1) < ROPE
    for j in range(heads // 2):
        tile = qr_ref[:, pl.ds(j * 128, 128)].astype(jnp.float32)
        rot32[pl.ds(2 * j, tokens, stride=heads), :] = jnp.where(low, tile, 0.0)
        rot32[pl.ds(2 * j + 1, tokens, stride=heads), :] = jnp.where(
            low, pltpu.roll(tile, 64, 1), 0.0
        )
    qv[:, pl.ds(LAT, 128)] = rot32[...].astype(jnp.bfloat16)

    for load in loads:
        load.wait()
    passed = {}

    def pass_on(k):
        forward[k].wait_recv()
        passed[k] = remote(
            kvr.at[PLACE[k], a], kvr.at[PLACE[k], a], p_send.at[k - 1], p_recv.at[k - 1], (c, sib)
        )
        passed[k].start()

    key_pos = [
        block_pos[2 * ctx_at(-ORDER[slot // 2]) + slot % 2] for slot in range(2 * SPAN)
    ]
    query_pos = [block_pos[2 * c], block_pos[2 * c + 1]]
    lane_row = lax.broadcasted_iota(jnp.int32, (64, CHUNK), 1)
    sub_row = lax.broadcasted_iota(jnp.int32, (64, CHUNK), 0)
    chunks = rows // CHUNK

    def score(group, i):
        first, count = GROUPS[group]
        at = pl.ds(i * CHUNK, CHUNK)
        keys = kvr[pl.ds(first, count)].reshape(count * 128, WIDE)
        s_buf = s_bufs[i % 2]
        s_buf[pl.ds(0, count * 128), :] = dot(keys, qv[at, :], NT)
        dp_buf[pl.ds(first * 128, count * 128), at] = dot(keys[:, :LAT], gv[at, :], NT)

    def soften(group, i):
        first, count = GROUPS[group]
        at = pl.ds(i * CHUNK, CHUNK)
        s_buf = s_bufs[i % 2]
        second = i * CHUNK // half
        ahead = lax.div(lane_row + (i * CHUNK - second * half), heads) - sub_row
        top = jnp.full((1, CHUNK), -1e30, jnp.float32)
        hidden = []
        for j in range(2 * count):
            part = pl.ds(j * 64, 64)
            s = s_buf[part, :]
            if 2 * first + j == second:
                s = jnp.where(ahead >= 0, s, -jnp.inf)
                s_buf[part, :] = s
                hidden.append(0.0)
            else:
                hidden.append(
                    jnp.where(key_pos[2 * first + j] < query_pos[second], 0.0, jnp.inf)
                )
            top = jnp.maximum(top, jnp.max(s, axis=0, keepdims=True) - hidden[j])
        total = jnp.zeros((1, CHUNK), jnp.float32)
        for j in range(2 * count):
            e = jnp.exp2((s_buf[pl.ds(j * 64, 64), :] - (top + hidden[j])) * SCALE_LOG2)
            e_buf[pl.ds(first * 128 + j * 64, 64), at] = e
            total = total + jnp.sum(e, axis=0, keepdims=True)
        tops[pl.ds(group, 1), at] = top
        sums[pl.ds(group, 1), at] = total

    def join(i):
        at = pl.ds(i * CHUNK, CHUNK)
        parts = range(len(GROUPS))
        top_of = [tops[pl.ds(g, 1), at] for g in parts]
        top = functools.reduce(jnp.maximum, top_of)
        part_of = [jnp.exp2((t - top) * SCALE_LOG2) for t in top_of]
        total = sum(f * sums[pl.ds(g, 1), at] for g, f in zip(parts, part_of))
        inv = 1.0 / total
        factor = []
        for g in parts:
            factor += [part_of[g] * inv] * (2 * GROUPS[g][1])
        delta = jnp.zeros((1, CHUNK), jnp.float32)
        for slot in range(2 * SPAN):
            part = pl.ds(slot * 64, 64)
            w = (e_buf[part, at] * factor[slot]).astype(jnp.bfloat16)
            w_t[part, at] = w
            delta = delta + jnp.sum(
                w.astype(jnp.float32) * dp_buf[part, at], axis=0, keepdims=True
            )
        for slot in range(2 * SPAN):
            part = pl.ds(slot * 64, 64)
            ds_t[part, at] = (
                (e_buf[part, at] * factor[slot]) * (dp_buf[part, at] - delta)
            ).astype(jnp.bfloat16)

    score(0, 0)
    for i in range(chunks):
        if i == 5:
            pass_on(1)
            pass_on(3)
        if i + 1 < chunks:
            score(0, i + 1)
        soften(0, i)
    passed[1].wait_recv()
    passed[3].wait_recv()
    score(1, 0)
    for i in range(chunks):
        if i == 4:
            pass_on(2)
        if i + 1 < chunks:
            score(1, i + 1)
        soften(1, i)
    passed[2].wait_recv()
    score(2, 0)
    for i in range(chunks):
        if i + 1 < chunks:
            score(2, i + 1)
        soften(2, i)
        join(i)

    d, asb, arb, bsb, brb = (d0, d1), (as0, as1), (ar0, ar1), (bs0, bs1), (br0, br1)
    csb, crb = (cs0, cs1), (cr0, cr1)

    def key_grads(n, first_place, count):
        first, width = SPLITS[n]
        at = pl.ds(first_place * 128, count * 128)
        slots = pl.ds(2 * first_place, 2 * count)
        shape = (2 * count, 2, 32)
        part = SCALE * dot(ds_t[at, :], qv[:, pl.ds(first, width)])
        latent = min(width, LAT - first)
        other = dot(w_t[at, :], gv[:, pl.ds(first, latent)])
        d[n][slots, :, :, pl.ds(0, latent)] = (part[:, :latent] + other).reshape(shape + (latent,))
        if latent < width:
            d[n][slots, :, :, pl.ds(latent, width - latent)] = part[:, latent:].reshape(
                shape + (width - latent,)
            )
        asb[n][slots] = d[n][slots, pl.ds(1 - a, 1)].reshape(2 * count, 32, width).astype(
            jnp.bfloat16
        )
        far = min(first_place, 1)
        copy = remote(
            asb[n].at[slots], arb[n].at[slots], a_send.at[n, far], a_recv.at[n, far], (c, sib)
        )
        copy.start()
        return copy

    def own(n, k):
        width = SPLITS[n][1]
        return d[n][pl.ds(2 * PLACE[k], 2), pl.ds(a, 1)].reshape(2, 32, width)

    def add_cores(n, copy):
        copy.wait_recv()
        sends = []
        for k in (2, 1, 3):
            got = arb[n][pl.ds(2 * PLACE[k], 2)].astype(jnp.float32)
            bsb[n][k - 1] = (own(n, k) + got).astype(jnp.bfloat16)
            sends.append(remote(
                bsb[n].at[k - 1], brb[n].at[k - 1], b_send.at[n, k - 1], b_recv.at[n, k - 1],
                (ctx_at(-k), h),
            ))
            sends[-1].start()
        return sends

    def add_context(n, near, sends):
        for copy in [near, *sends]:
            copy.wait_recv()
        added = own(n, 0) + arb[n][pl.ds(0, 2)].astype(jnp.float32)
        for k in (1, 2, 3):
            added = added + brb[n][k - 1].astype(jnp.float32)
        width = SPLITS[n][1]
        d[n][pl.ds(0, 2), pl.ds(a, 1)] = added.reshape(2, 1, 32, width)
        csb[n][...] = d[n][pl.ds(1 - z, 1), pl.ds(a, 1)].reshape(32, width).astype(jnp.bfloat16)
        copy = remote(csb[n], crb[n], c_send.at[n], c_recv.at[n], (c, zpart))
        copy.start()
        return copy

    def finish(n, copy):
        copy.wait_recv()
        first, width = SPLITS[n]
        result = d[n][pl.ds(z, 1), pl.ds(a, 1)].reshape(32, width) + crb[n][...].astype(jnp.float32)
        result = result.astype(jnp.bfloat16)
        latent = min(width, LAT - first)
        dkv_ref[:, pl.ds(first, latent)] = result[:, :latent]
        if latent < width:
            dkr_ref[...] = result[:, latent:latent + ROPE]

    def query_grads(i):
        start = i * CHUNK
        at = pl.ds(start, CHUNK)
        keys = kvr[...].reshape(SPAN * 128, WIDE)
        grad = SCALE * dot(ds_t[:, at], keys, TN)
        dq_ref[at, :] = grad[:, :LAT].astype(jnp.bfloat16)
        rot32[at, :] = grad[:, LAT:]

    a0 = key_grads(0, 1, 3)
    a1 = key_grads(1, 1, 3)
    b0 = add_cores(0, a0)
    n0 = key_grads(0, 0, 1)
    b1 = add_cores(1, a1)
    n1 = key_grads(1, 0, 1)
    for i in range(chunks):
        query_grads(i)

    for j in range(heads // 2):
        even = rot32[pl.ds(2 * j, tokens, stride=heads), :]
        odd = rot32[pl.ds(2 * j + 1, tokens, stride=heads), :]
        dqr_ref[:, pl.ds(j * 128, 128)] = jnp.where(
            low, even, pltpu.roll(odd, 64, 1)
        ).astype(jnp.bfloat16)

    c0 = add_context(0, n0, b0)
    c1 = add_context(1, n1, b1)
    finish(0, c0)
    for copy in [*forward.values(), *passed.values(), a0, a1, n0, n1, *b0, *b1, c0]:
        copy.wait_send()
    finish(1, c1)
    c1.wait_send()


def move(*refs):
    sources, targets, sem = refs[:4], refs[4:8], refs[8]
    rows = sources[0].shape[0] // PIECES
    copies = [
        pltpu.make_async_copy(
            sources[0].at[pl.ds(i * rows, rows)], targets[0].at[pl.ds(i * rows, rows)], sem.at[i]
        )
        for i in range(PIECES)
    ]
    copies += [
        pltpu.make_async_copy(sources[i], targets[i], sem.at[PIECES + i - 1]) for i in (1, 2, 3)
    ]
    for copy in copies:
        copy.start()
    for copy in copies:
        copy.wait()


def per_device(q_latent, q_rope, kv_latent, k_rope, out_grad, block_pos):
    tokens, heads, lat = q_latent.shape
    rows = tokens * heads
    keys = SPAN * tokens
    n_ctx = lax.axis_size("ctx")
    bf16, f32 = jnp.bfloat16, jnp.float32
    vmem = pl.BlockSpec(memory_space=pltpu.VMEM)
    hbm = pl.BlockSpec(memory_space=pltpu.HBM)
    widths = [width for _, width in SPLITS]

    def pairs(shape, kind):
        return [pltpu.VMEM(shape + (width,), kind) for width in widths]

    dma = pltpu.SemaphoreType.DMA
    scratch = [
        pltpu.SMEM(block_pos.shape, jnp.int32),
        pltpu.VMEM((tokens, lat), bf16),
        pltpu.VMEM((ROPE, tokens), bf16),
        pltpu.VMEM((tokens, heads * ROPE), bf16),
        pltpu.VMEM((SPAN, 2, 64, WIDE), bf16),
        pltpu.VMEM((rows, WIDE), bf16),
        pltpu.VMEM((rows, lat), bf16),
        pltpu.VMEM((rows, 128), f32),
        *[pltpu.VMEM((keys // 2, CHUNK), f32) for _ in range(2)],
        *[pltpu.VMEM((keys, rows), f32) for _ in range(2)],
        *[pltpu.VMEM((8, rows), f32) for _ in range(2)],
        pltpu.VMEM((keys, rows), bf16),
        pltpu.VMEM((keys, rows), bf16),
        *pairs((2 * SPAN, 2, 32), f32),
        *pairs((2 * SPAN, 32), bf16),
        *pairs((2 * SPAN, 32), bf16),
        *pairs((3, 2, 32), bf16),
        *pairs((3, 2, 32), bf16),
        *pairs((32,), bf16),
        *pairs((32,), bf16),
        dma((6,)),
        dma((3,)), dma((3,)), dma((3,)), dma((3,)),
        dma((2, 2)), dma((2, 2)), dma((2, 3)), dma((2, 3)), dma((2,)), dma((2,)),
    ]
    macs = rows * keys * (WIDE * 3 + 2 * lat)
    dq, dqr, dkv, dkr = pl.pallas_call(
        functools.partial(kernel, n_ctx, heads),
        out_shape=(
            pltpu.VMEM((rows, lat), bf16),
            pltpu.VMEM((tokens, heads * ROPE), bf16),
            pltpu.VMEM((tokens // 4, lat), bf16),
            pltpu.VMEM((tokens // 4, ROPE), bf16),
        ),
        in_specs=[hbm] * 6,
        out_specs=(vmem,) * 4,
        scratch_shapes=scratch,
        compiler_params=pltpu.CompilerParams(
            collective_id=0, has_side_effects=True, vmem_limit_bytes=56 * 2**20
        ),
        cost_estimate=pl.CostEstimate(
            flops=2 * macs, bytes_accessed=7 * 2**20, transcendentals=rows * keys
        ),
    )(
        block_pos, kv_latent, k_rope.T, q_rope,
        q_latent.reshape(rows, lat), out_grad.reshape(rows, lat),
    )
    results = (dq, dqr, dkv, dkr)
    dq, dqr, dkv, dkr = pl.pallas_call(
        move,
        out_shape=tuple(jax.ShapeDtypeStruct(r.shape, r.dtype) for r in results),
        in_specs=[vmem] * 4,
        out_specs=(hbm,) * 4,
        scratch_shapes=[dma((PIECES + 3,))],
        compiler_params=pltpu.CompilerParams(vmem_limit_bytes=2**20),
    )(*results)
    return dq.reshape(tokens, heads, lat), dqr, dkv, dkr


def solution(mesh):
    in_specs = (
        P("ctx", "head", None),
        P("ctx", "head"),
        P("ctx", None),
        P("ctx", None),
        P("ctx", "head", None),
        P(),
    )
    out_specs = (
        P("ctx", "head", None),
        P("ctx", "head"),
        P(("ctx", "head"), None),
        P(("ctx", "head"), None),
    )
    return jax.shard_map(
        per_device, mesh=mesh, in_specs=in_specs, out_specs=out_specs, check_vma=False
    )
```

```python
import functools

import jax
import jax.numpy as jnp
from jax import lax
from jax.experimental import pallas as pl
from jax.experimental.pallas import tpu as pltpu
from jax.sharding import PartitionSpec as P

SPAN = 4
LAT = 512
ROPE = 64
WIDE = 640
SCALE = 192.0 ** (-0.5)
SCALE_LOG2 = SCALE * 1.4426950408889634
CHUNK = 256
ORDER = (0, 1, 3, 2)
PLACE = tuple(ORDER.index(k) for k in range(SPAN))
GROUPS = ((0, 1), (1, 2), (3, 1))
SPLITS = ((0, 256), (256, 384))

PIECES = 8

NT = (((1,), (1,)), ((), ()))
TN = (((0,), (0,)), ((), ()))


def dot(a, b, dims=(((1,), (0,)), ((), ()))):
    return lax.dot_general(a, b, dims, preferred_element_type=jnp.float32)


def kernel(
    n_ctx, heads,
    pos_hbm, kv_hbm, kr_hbm, qr_hbm, q_hbm, g_hbm,
    dq_ref, dqr_ref, dkv_ref, dkr_ref,
    block_pos, kv_ref, kr_ref, qr_ref, kvr, qv, gv, rot32, s_a, s_b, e_buf, dp_buf, tops, sums, ds_t, w_t,
    d0, d1, as0, as1, ar0, ar1, bs0, bs1, br0, br1, cs0, cs1, cr0, cr1,
    in_sem, f_send, f_recv, p_send, p_recv,
    a_send, a_recv, b_send, b_recv, c_send, c_recv,
):
    c = lax.axis_index("ctx")
    h = lax.axis_index("head")
    z = lax.div(h, 2)
    a = lax.rem(h, 2)
    sib = z * 2 + (1 - a)
    zpart = (1 - z) * 2 + a
    rows = qv.shape[0]
    half = rows // 2
    s_bufs = (s_a, s_b)

    def ctx_at(k):
        return lax.rem(c + k + n_ctx, n_ctx)

    load_keys = [
        pltpu.make_async_copy(kv_hbm, kv_ref, in_sem.at[0]),
        pltpu.make_async_copy(kr_hbm, kr_ref, in_sem.at[1]),
    ]
    load_rot = pltpu.make_async_copy(qr_hbm, qr_ref, in_sem.at[2])
    loads = [
        pltpu.make_async_copy(pos_hbm, block_pos, in_sem.at[3]),
        pltpu.make_async_copy(q_hbm, qv.at[:, pl.ds(0, LAT)], in_sem.at[4]),
        pltpu.make_async_copy(g_hbm, gv, in_sem.at[5]),
    ]
    barrier = pltpu.get_barrier_semaphore()
    peers = [(ctx_at(k), h) for k in (-3, -2, -1, 3, 2, 1)] + [(c, sib), (c, zpart)]
    for peer in peers:
        pl.semaphore_signal(barrier, inc=1, device_id=peer, device_id_type=pl.DeviceIdType.MESH)

    for load in [*load_keys, load_rot, *loads]:
        load.start()

    for load in load_keys:
        load.wait()
    kvr[0, :, :, pl.ds(0, LAT)] = kv_ref[...].reshape(2, 64, LAT)
    rot = kr_ref[...].astype(jnp.float32)
    kvr[0, :, :, pl.ds(LAT, 128)] = jnp.concatenate(
        [rot, jnp.zeros_like(rot)], axis=0
    ).T.astype(jnp.bfloat16).reshape(2, 64, 128)

    pl.semaphore_wait(barrier, len(peers))

    def remote(src, dst, send, recv, peer):
        return pltpu.make_async_remote_copy(
            src_ref=src, dst_ref=dst, send_sem=send, recv_sem=recv,
            device_id=peer, device_id_type=pl.DeviceIdType.MESH,
        )

    forward = {}
    for k in (1, 3, 2):
        forward[k] = remote(
            kvr.at[0, a], kvr.at[PLACE[k], a], f_send.at[k - 1], f_recv.at[k - 1], (ctx_at(k), h)
        )
        forward[k].start()

    load_rot.wait()
    tokens = qr_ref.shape[0]
    low = lax.broadcasted_iota(jnp.int32, (tokens, 128), 1) < ROPE
    for j in range(heads // 2):
        tile = qr_ref[:, pl.ds(j * 128, 128)].astype(jnp.float32)
        rot32[pl.ds(2 * j, tokens, stride=heads), :] = jnp.where(low, tile, 0.0)
        rot32[pl.ds(2 * j + 1, tokens, stride=heads), :] = jnp.where(
            low, pltpu.roll(tile, 64, 1), 0.0
        )
    qv[:, pl.ds(LAT, 128)] = rot32[...].astype(jnp.bfloat16)

    for load in loads:
        load.wait()
    passed = {}

    def pass_on(k):
        forward[k].wait_recv()
        passed[k] = remote(
            kvr.at[PLACE[k], a], kvr.at[PLACE[k], a], p_send.at[k - 1], p_recv.at[k - 1], (c, sib)
        )
        passed[k].start()

    key_pos = [
        block_pos[2 * ctx_at(-ORDER[slot // 2]) + slot % 2] for slot in range(2 * SPAN)
    ]
    query_pos = [block_pos[2 * c], block_pos[2 * c + 1]]
    lane_row = lax.broadcasted_iota(jnp.int32, (64, CHUNK), 1)
    sub_row = lax.broadcasted_iota(jnp.int32, (64, CHUNK), 0)
    chunks = rows // CHUNK

    def score(group, i):
        first, count = GROUPS[group]
        at = pl.ds(i * CHUNK, CHUNK)
        keys = kvr[pl.ds(first, count)].reshape(count * 128, WIDE)
        s_buf = s_bufs[i % 2]
        s_buf[pl.ds(0, count * 128), :] = dot(keys, qv[at, :], NT)
        dp_buf[pl.ds(first * 128, count * 128), at] = dot(keys[:, :LAT], gv[at, :], NT)

    def soften(group, i):
        first, count = GROUPS[group]
        at = pl.ds(i * CHUNK, CHUNK)
        s_buf = s_bufs[i % 2]
        second = i * CHUNK // half
        ahead = lax.div(lane_row + (i * CHUNK - second * half), heads) - sub_row
        top = jnp.full((1, CHUNK), -1e30, jnp.float32)
        hidden = []
        for j in range(2 * count):
            part = pl.ds(j * 64, 64)
            s = s_buf[part, :]
            if 2 * first + j == second:
                s = jnp.where(ahead >= 0, s, -jnp.inf)
                s_buf[part, :] = s
                hidden.append(0.0)
            else:
                hidden.append(
                    jnp.where(key_pos[2 * first + j] < query_pos[second], 0.0, jnp.inf)
                )
            top = jnp.maximum(top, jnp.max(s, axis=0, keepdims=True) - hidden[j])
        total = jnp.zeros((1, CHUNK), jnp.float32)
        for j in range(2 * count):
            e = jnp.exp2((s_buf[pl.ds(j * 64, 64), :] - (top + hidden[j])) * SCALE_LOG2)
            e_buf[pl.ds(first * 128 + j * 64, 64), at] = e
            total = total + jnp.sum(e, axis=0, keepdims=True)
        tops[pl.ds(group, 1), at] = top
        sums[pl.ds(group, 1), at] = total

    def join(i):
        at = pl.ds(i * CHUNK, CHUNK)
        parts = range(len(GROUPS))
        top_of = [tops[pl.ds(g, 1), at] for g in parts]
        top = functools.reduce(jnp.maximum, top_of)
        part_of = [jnp.exp2((t - top) * SCALE_LOG2) for t in top_of]
        total = sum(f * sums[pl.ds(g, 1), at] for g, f in zip(parts, part_of))
        inv = 1.0 / total
        factor = []
        for g in parts:
            factor += [part_of[g] * inv] * (2 * GROUPS[g][1])
        delta = jnp.zeros((1, CHUNK), jnp.float32)
        for slot in range(2 * SPAN):
            part = pl.ds(slot * 64, 64)
            w = (e_buf[part, at] * factor[slot]).astype(jnp.bfloat16)
            w_t[part, at] = w
            delta = delta + jnp.sum(
                w.astype(jnp.float32) * dp_buf[part, at], axis=0, keepdims=True
            )
        for slot in range(2 * SPAN):
            part = pl.ds(slot * 64, 64)
            ds_t[part, at] = (
                (e_buf[part, at] * factor[slot]) * (dp_buf[part, at] - delta)
            ).astype(jnp.bfloat16)

    score(0, 0)
    for i in range(chunks):
        if i == 5:
            pass_on(1)
            pass_on(3)
        if i + 1 < chunks:
            score(0, i + 1)
        soften(0, i)
    passed[1].wait_recv()
    passed[3].wait_recv()
    score(1, 0)
    for i in range(chunks):
        if i == 4:
            pass_on(2)
        if i + 1 < chunks:
            score(1, i + 1)
        soften(1, i)
    passed[2].wait_recv()
    score(2, 0)
    for i in range(chunks):
        if i + 1 < chunks:
            score(2, i + 1)
        soften(2, i)
        join(i)

    d, asb, arb, bsb, brb = (d0, d1), (as0, as1), (ar0, ar1), (bs0, bs1), (br0, br1)
    csb, crb = (cs0, cs1), (cr0, cr1)

    def key_grads(n, first_place, count):
        first, width = SPLITS[n]
        at = pl.ds(first_place * 128, count * 128)
        slots = pl.ds(2 * first_place, 2 * count)
        shape = (2 * count, 2, 32)
        part = SCALE * dot(ds_t[at, :], qv[:, pl.ds(first, width)])
        latent = min(width, LAT - first)
        other = dot(w_t[at, :], gv[:, pl.ds(first, latent)])
        d[n][slots, :, :, pl.ds(0, latent)] = (part[:, :latent] + other).reshape(shape + (latent,))
        if latent < width:
            d[n][slots, :, :, pl.ds(latent, width - latent)] = part[:, latent:].reshape(
                shape + (width - latent,)
            )
        asb[n][slots] = d[n][slots, pl.ds(1 - a, 1)].reshape(2 * count, 32, width).astype(
            jnp.bfloat16
        )
        far = min(first_place, 1)
        copy = remote(
            asb[n].at[slots], arb[n].at[slots], a_send.at[n, far], a_recv.at[n, far], (c, sib)
        )
        copy.start()
        return copy

    def own(n, k):
        width = SPLITS[n][1]
        return d[n][pl.ds(2 * PLACE[k], 2), pl.ds(a, 1)].reshape(2, 32, width)

    def add_cores(n, copy):
        copy.wait_recv()
        sends = []
        for k in (2, 1, 3):
            got = arb[n][pl.ds(2 * PLACE[k], 2)].astype(jnp.float32)
            bsb[n][k - 1] = (own(n, k) + got).astype(jnp.bfloat16)
            sends.append(remote(
                bsb[n].at[k - 1], brb[n].at[k - 1], b_send.at[n, k - 1], b_recv.at[n, k - 1],
                (ctx_at(-k), h),
            ))
            sends[-1].start()
        return sends

    def add_context(n, near, sends):
        for copy in [near, *sends]:
            copy.wait_recv()
        added = own(n, 0) + arb[n][pl.ds(0, 2)].astype(jnp.float32)
        for k in (1, 2, 3):
            added = added + brb[n][k - 1].astype(jnp.float32)
        width = SPLITS[n][1]
        d[n][pl.ds(0, 2), pl.ds(a, 1)] = added.reshape(2, 1, 32, width)
        csb[n][...] = d[n][pl.ds(1 - z, 1), pl.ds(a, 1)].reshape(32, width).astype(jnp.bfloat16)
        copy = remote(csb[n], crb[n], c_send.at[n], c_recv.at[n], (c, zpart))
        copy.start()
        return copy

    def finish(n, copy):
        copy.wait_recv()
        first, width = SPLITS[n]
        result = d[n][pl.ds(z, 1), pl.ds(a, 1)].reshape(32, width) + crb[n][...].astype(jnp.float32)
        result = result.astype(jnp.bfloat16)
        latent = min(width, LAT - first)
        dkv_ref[:, pl.ds(first, latent)] = result[:, :latent]
        if latent < width:
            dkr_ref[...] = result[:, latent:latent + ROPE]

    def query_grads(i):
        start = i * CHUNK
        at = pl.ds(start, CHUNK)
        keys = kvr[...].reshape(SPAN * 128, WIDE)
        grad = SCALE * dot(ds_t[:, at], keys, TN)
        dq_ref[at, :] = grad[:, :LAT].astype(jnp.bfloat16)
        rot32[at, :] = grad[:, LAT:]

    a0 = key_grads(0, 1, 3)
    a1 = key_grads(1, 1, 3)
    b0 = add_cores(0, a0)
    n0 = key_grads(0, 0, 1)
    b1 = add_cores(1, a1)
    n1 = key_grads(1, 0, 1)
    for i in range(chunks):
        query_grads(i)

    for j in range(heads // 2):
        even = rot32[pl.ds(2 * j, tokens, stride=heads), :]
        odd = rot32[pl.ds(2 * j + 1, tokens, stride=heads), :]
        dqr_ref[:, pl.ds(j * 128, 128)] = jnp.where(
            low, even, pltpu.roll(odd, 64, 1)
        ).astype(jnp.bfloat16)

    c0 = add_context(0, n0, b0)
    c1 = add_context(1, n1, b1)
    finish(0, c0)
    for copy in [*forward.values(), *passed.values(), a0, a1, n0, n1, *b0, *b1, c0]:
        copy.wait_send()
    finish(1, c1)
    c1.wait_send()


def move(*refs):
    sources, targets, sem = refs[:4], refs[4:8], refs[8]
    rows = sources[0].shape[0] // PIECES
    copies = [
        pltpu.make_async_copy(
            sources[0].at[pl.ds(i * rows, rows)], targets[0].at[pl.ds(i * rows, rows)], sem.at[i]
        )
        for i in range(PIECES)
    ]
    copies += [
        pltpu.make_async_copy(sources[i], targets[i], sem.at[PIECES + i - 1]) for i in (1, 2, 3)
    ]
    for copy in copies:
        copy.start()
    for copy in copies:
        copy.wait()


def per_device(q_latent, q_rope, kv_latent, k_rope, out_grad, block_pos):
    tokens, heads, lat = q_latent.shape
    rows = tokens * heads
    keys = SPAN * tokens
    n_ctx = lax.axis_size("ctx")
    bf16, f32 = jnp.bfloat16, jnp.float32
    vmem = pl.BlockSpec(memory_space=pltpu.VMEM)
    hbm = pl.BlockSpec(memory_space=pltpu.HBM)
    widths = [width for _, width in SPLITS]

    def pairs(shape, kind):
        return [pltpu.VMEM(shape + (width,), kind) for width in widths]

    dma = pltpu.SemaphoreType.DMA
    scratch = [
        pltpu.SMEM(block_pos.shape, jnp.int32),
        pltpu.VMEM((tokens, lat), bf16),
        pltpu.VMEM((ROPE, tokens), bf16),
        pltpu.VMEM((tokens, heads * ROPE), bf16),
        pltpu.VMEM((SPAN, 2, 64, WIDE), bf16),
        pltpu.VMEM((rows, WIDE), bf16),
        pltpu.VMEM((rows, lat), bf16),
        pltpu.VMEM((rows, 128), f32),
        *[pltpu.VMEM((keys // 2, CHUNK), f32) for _ in range(2)],
        *[pltpu.VMEM((keys, rows), f32) for _ in range(2)],
        *[pltpu.VMEM((8, rows), f32) for _ in range(2)],
        pltpu.VMEM((keys, rows), bf16),
        pltpu.VMEM((keys, rows), bf16),
        *pairs((2 * SPAN, 2, 32), f32),
        *pairs((2 * SPAN, 32), bf16),
        *pairs((2 * SPAN, 32), bf16),
        *pairs((3, 2, 32), bf16),
        *pairs((3, 2, 32), bf16),
        *pairs((32,), bf16),
        *pairs((32,), bf16),
        dma((6,)),
        dma((3,)), dma((3,)), dma((3,)), dma((3,)),
        dma((2, 2)), dma((2, 2)), dma((2, 3)), dma((2, 3)), dma((2,)), dma((2,)),
    ]
    macs = rows * keys * (WIDE * 3 + 2 * lat)
    dq, dqr, dkv, dkr = pl.pallas_call(
        functools.partial(kernel, n_ctx, heads),
        out_shape=(
            pltpu.VMEM((rows, lat), bf16),
            pltpu.VMEM((tokens, heads * ROPE), bf16),
            pltpu.VMEM((tokens // 4, lat), bf16),
            pltpu.VMEM((tokens // 4, ROPE), bf16),
        ),
        in_specs=[hbm] * 6,
        out_specs=(vmem,) * 4,
        scratch_shapes=scratch,
        compiler_params=pltpu.CompilerParams(
            collective_id=0, has_side_effects=True, vmem_limit_bytes=56 * 2**20
        ),
        cost_estimate=pl.CostEstimate(
            flops=2 * macs, bytes_accessed=7 * 2**20, transcendentals=rows * keys
        ),
    )(
        block_pos, kv_latent, k_rope.T, q_rope,
        q_latent.reshape(rows, lat), out_grad.reshape(rows, lat),
    )
    results = (dq, dqr, dkv, dkr)
    dq, dqr, dkv, dkr = pl.pallas_call(
        move,
        out_shape=tuple(jax.ShapeDtypeStruct(r.shape, r.dtype) for r in results),
        in_specs=[vmem] * 4,
        out_specs=(hbm,) * 4,
        scratch_shapes=[dma((PIECES + 3,))],
        compiler_params=pltpu.CompilerParams(vmem_limit_bytes=2**20),
    )(*results)
    return dq.reshape(tokens, heads, lat), dqr, dkv, dkr


def solution(mesh):
    in_specs = (
        P("ctx", "head", None),
        P("ctx", "head"),
        P("ctx", None),
        P("ctx", None),
        P("ctx", "head", None),
        P(),
    )
    out_specs = (
        P("ctx", "head", None),
        P("ctx", "head"),
        P(("ctx", "head"), None),
        P(("ctx", "head"), None),
    )
    return jax.shard_map(
        per_device, mesh=mesh, in_specs=in_specs, out_specs=out_specs, check_vma=False
    )
```

```python
import functools

import jax
import jax.numpy as jnp
from jax import lax
from jax.experimental import pallas as pl
from jax.experimental.pallas import tpu as pltpu
from jax.sharding import PartitionSpec as P

SPAN = 4
LAT = 512
ROPE = 64
WIDE = 640
SCALE = 192.0 ** (-0.5)
SCALE_LOG2 = SCALE * 1.4426950408889634
CHUNK = 256
ORDER = (0, 1, 3, 2)
PLACE = tuple(ORDER.index(k) for k in range(SPAN))
GROUPS = ((0, 1), (1, 3))
SPLITS = ((0, 256), (256, 384))

PIECES = 8

NT = (((1,), (1,)), ((), ()))
TN = (((0,), (0,)), ((), ()))


def dot(a, b, dims=(((1,), (0,)), ((), ()))):
    return lax.dot_general(a, b, dims, preferred_element_type=jnp.float32)


def kernel(
    n_ctx, heads,
    pos_hbm, kv_hbm, kr_hbm, qr_hbm, q_hbm, g_hbm,
    dq_ref, dqr_ref, dkv_ref, dkr_ref,
    block_pos, kv_ref, kr_ref, qr_ref, kvr, qv, gv, rot32, s_a, s_b, e_buf, dp_buf, tops, sums, ds_t, w_t,
    d0, d1, as0, as1, ar0, ar1, bs0, bs1, br0, br1, cs0, cs1, cr0, cr1,
    in_sem, f_send, f_recv, p_send, p_recv,
    a_send, a_recv, b_send, b_recv, c_send, c_recv,
):
    c = lax.axis_index("ctx")
    h = lax.axis_index("head")
    z = lax.div(h, 2)
    a = lax.rem(h, 2)
    sib = z * 2 + (1 - a)
    zpart = (1 - z) * 2 + a
    rows = qv.shape[0]
    half = rows // 2
    s_bufs = (s_a, s_b)

    def ctx_at(k):
        return lax.rem(c + k + n_ctx, n_ctx)

    load_keys = [
        pltpu.make_async_copy(kv_hbm, kv_ref, in_sem.at[0]),
        pltpu.make_async_copy(kr_hbm, kr_ref, in_sem.at[1]),
    ]
    load_rot = pltpu.make_async_copy(qr_hbm, qr_ref, in_sem.at[2])
    loads = [
        pltpu.make_async_copy(pos_hbm, block_pos, in_sem.at[3]),
        pltpu.make_async_copy(q_hbm, qv.at[:, pl.ds(0, LAT)], in_sem.at[4]),
        pltpu.make_async_copy(g_hbm, gv, in_sem.at[5]),
    ]
    barrier = pltpu.get_barrier_semaphore()
    peers = [(ctx_at(k), h) for k in (-3, -2, -1, 3, 2, 1)] + [(c, sib), (c, zpart)]
    for peer in peers:
        pl.semaphore_signal(barrier, inc=1, device_id=peer, device_id_type=pl.DeviceIdType.MESH)

    for load in [*load_keys, load_rot, *loads]:
        load.start()

    for load in load_keys:
        load.wait()
    kvr[0, :, :, pl.ds(0, LAT)] = kv_ref[...].reshape(2, 64, LAT)
    rot = kr_ref[...].astype(jnp.float32)
    kvr[0, :, :, pl.ds(LAT, 128)] = jnp.concatenate(
        [rot, jnp.zeros_like(rot)], axis=0
    ).T.astype(jnp.bfloat16).reshape(2, 64, 128)

    pl.semaphore_wait(barrier, len(peers))

    def remote(src, dst, send, recv, peer):
        return pltpu.make_async_remote_copy(
            src_ref=src, dst_ref=dst, send_sem=send, recv_sem=recv,
            device_id=peer, device_id_type=pl.DeviceIdType.MESH,
        )

    forward = {}
    for k in (1, 3, 2):
        forward[k] = remote(
            kvr.at[0, a], kvr.at[PLACE[k], a], f_send.at[k - 1], f_recv.at[k - 1], (ctx_at(k), h)
        )
        forward[k].start()

    load_rot.wait()
    tokens = qr_ref.shape[0]
    low = lax.broadcasted_iota(jnp.int32, (tokens, 128), 1) < ROPE
    for j in range(heads // 2):
        tile = qr_ref[:, pl.ds(j * 128, 128)].astype(jnp.float32)
        rot32[pl.ds(2 * j, tokens, stride=heads), :] = jnp.where(low, tile, 0.0)
        rot32[pl.ds(2 * j + 1, tokens, stride=heads), :] = jnp.where(
            low, pltpu.roll(tile, 64, 1), 0.0
        )
    qv[:, pl.ds(LAT, 128)] = rot32[...].astype(jnp.bfloat16)

    for load in loads:
        load.wait()
    passed = {}

    def pass_on(k):
        forward[k].wait_recv()
        passed[k] = remote(
            kvr.at[PLACE[k], a], kvr.at[PLACE[k], a], p_send.at[k - 1], p_recv.at[k - 1], (c, sib)
        )
        passed[k].start()

    key_pos = [
        block_pos[2 * ctx_at(-ORDER[slot // 2]) + slot % 2] for slot in range(2 * SPAN)
    ]
    query_pos = [block_pos[2 * c], block_pos[2 * c + 1]]
    lane_row = lax.broadcasted_iota(jnp.int32, (64, CHUNK), 1)
    sub_row = lax.broadcasted_iota(jnp.int32, (64, CHUNK), 0)
    chunks = rows // CHUNK

    def score(group, i):
        first, count = GROUPS[group]
        at = pl.ds(i * CHUNK, CHUNK)
        keys = kvr[pl.ds(first, count)].reshape(count * 128, WIDE)
        s_buf = s_bufs[i % 2]
        s_buf[pl.ds(0, count * 128), :] = dot(keys, qv[at, :], NT)
        dp_buf[pl.ds(first * 128, count * 128), at] = dot(keys[:, :LAT], gv[at, :], NT)

    def soften(group, i):
        first, count = GROUPS[group]
        at = pl.ds(i * CHUNK, CHUNK)
        s_buf = s_bufs[i % 2]
        second = i * CHUNK // half
        ahead = lax.div(lane_row + (i * CHUNK - second * half), heads) - sub_row
        top = jnp.full((1, CHUNK), -1e30, jnp.float32)
        hidden = []
        for j in range(2 * count):
            part = pl.ds(j * 64, 64)
            s = s_buf[part, :]
            if 2 * first + j == second:
                s = jnp.where(ahead >= 0, s, -jnp.inf)
                s_buf[part, :] = s
                hidden.append(0.0)
            else:
                hidden.append(
                    jnp.where(key_pos[2 * first + j] < query_pos[second], 0.0, jnp.inf)
                )
            top = jnp.maximum(top, jnp.max(s, axis=0, keepdims=True) - hidden[j])
        total = jnp.zeros((1, CHUNK), jnp.float32)
        for j in range(2 * count):
            e = jnp.exp2((s_buf[pl.ds(j * 64, 64), :] - (top + hidden[j])) * SCALE_LOG2)
            e_buf[pl.ds(first * 128 + j * 64, 64), at] = e
            total = total + jnp.sum(e, axis=0, keepdims=True)
        tops[pl.ds(group, 1), at] = top
        sums[pl.ds(group, 1), at] = total

    def join(i):
        at = pl.ds(i * CHUNK, CHUNK)
        parts = range(len(GROUPS))
        top_of = [tops[pl.ds(g, 1), at] for g in parts]
        top = functools.reduce(jnp.maximum, top_of)
        part_of = [jnp.exp2((t - top) * SCALE_LOG2) for t in top_of]
        total = sum(f * sums[pl.ds(g, 1), at] for g, f in zip(parts, part_of))
        inv = 1.0 / total
        factor = []
        for g in parts:
            factor += [part_of[g] * inv] * (2 * GROUPS[g][1])
        delta = jnp.zeros((1, CHUNK), jnp.float32)
        for slot in range(2 * SPAN):
            part = pl.ds(slot * 64, 64)
            w = (e_buf[part, at] * factor[slot]).astype(jnp.bfloat16)
            w_t[part, at] = w
            delta = delta + jnp.sum(
                w.astype(jnp.float32) * dp_buf[part, at], axis=0, keepdims=True
            )
        for slot in range(2 * SPAN):
            part = pl.ds(slot * 64, 64)
            ds_t[part, at] = (
                (e_buf[part, at] * factor[slot]) * (dp_buf[part, at] - delta)
            ).astype(jnp.bfloat16)

    score(0, 0)
    for i in range(chunks):
        if i == 5:
            pass_on(1)
            pass_on(3)
        if i + 1 < chunks:
            score(0, i + 1)
        soften(0, i)
    pass_on(2)
    passed[1].wait_recv()
    passed[3].wait_recv()
    passed[2].wait_recv()
    score(1, 0)
    for i in range(chunks):
        if i + 1 < chunks:
            score(1, i + 1)
        soften(1, i)
        join(i)

    d, asb, arb, bsb, brb = (d0, d1), (as0, as1), (ar0, ar1), (bs0, bs1), (br0, br1)
    csb, crb = (cs0, cs1), (cr0, cr1)

    def key_grads(n, first_place, count):
        first, width = SPLITS[n]
        at = pl.ds(first_place * 128, count * 128)
        slots = pl.ds(2 * first_place, 2 * count)
        shape = (2 * count, 2, 32)
        part = SCALE * dot(ds_t[at, :], qv[:, pl.ds(first, width)])
        latent = min(width, LAT - first)
        other = dot(w_t[at, :], gv[:, pl.ds(first, latent)])
        d[n][slots, :, :, pl.ds(0, latent)] = (part[:, :latent] + other).reshape(shape + (latent,))
        if latent < width:
            d[n][slots, :, :, pl.ds(latent, width - latent)] = part[:, latent:].reshape(
                shape + (width - latent,)
            )
        asb[n][slots] = d[n][slots, pl.ds(1 - a, 1)].reshape(2 * count, 32, width).astype(
            jnp.bfloat16
        )
        far = min(first_place, 1)
        copy = remote(
            asb[n].at[slots], arb[n].at[slots], a_send.at[n, far], a_recv.at[n, far], (c, sib)
        )
        copy.start()
        return copy

    def own(n, k):
        width = SPLITS[n][1]
        return d[n][pl.ds(2 * PLACE[k], 2), pl.ds(a, 1)].reshape(2, 32, width)

    def add_cores(n, copy):
        copy.wait_recv()
        sends = []
        for k in (2, 1, 3):
            got = arb[n][pl.ds(2 * PLACE[k], 2)].astype(jnp.float32)
            bsb[n][k - 1] = (own(n, k) + got).astype(jnp.bfloat16)
            sends.append(remote(
                bsb[n].at[k - 1], brb[n].at[k - 1], b_send.at[n, k - 1], b_recv.at[n, k - 1],
                (ctx_at(-k), h),
            ))
            sends[-1].start()
        return sends

    def add_context(n, near, sends):
        for copy in [near, *sends]:
            copy.wait_recv()
        added = own(n, 0) + arb[n][pl.ds(0, 2)].astype(jnp.float32)
        for k in (1, 2, 3):
            added = added + brb[n][k - 1].astype(jnp.float32)
        width = SPLITS[n][1]
        d[n][pl.ds(0, 2), pl.ds(a, 1)] = added.reshape(2, 1, 32, width)
        csb[n][...] = d[n][pl.ds(1 - z, 1), pl.ds(a, 1)].reshape(32, width).astype(jnp.bfloat16)
        copy = remote(csb[n], crb[n], c_send.at[n], c_recv.at[n], (c, zpart))
        copy.start()
        return copy

    def finish(n, copy):
        copy.wait_recv()
        first, width = SPLITS[n]
        result = d[n][pl.ds(z, 1), pl.ds(a, 1)].reshape(32, width) + crb[n][...].astype(jnp.float32)
        result = result.astype(jnp.bfloat16)
        latent = min(width, LAT - first)
        dkv_ref[:, pl.ds(first, latent)] = result[:, :latent]
        if latent < width:
            dkr_ref[...] = result[:, latent:latent + ROPE]

    def query_grads(i):
        start = i * CHUNK
        at = pl.ds(start, CHUNK)
        keys = kvr[...].reshape(SPAN * 128, WIDE)
        grad = SCALE * dot(ds_t[:, at], keys, TN)
        dq_ref[at, :] = grad[:, :LAT].astype(jnp.bfloat16)
        rot32[at, :] = grad[:, LAT:]

    a0 = key_grads(0, 1, 3)
    a1 = key_grads(1, 1, 3)
    b0 = add_cores(0, a0)
    n0 = key_grads(0, 0, 1)
    b1 = add_cores(1, a1)
    n1 = key_grads(1, 0, 1)
    for i in range(chunks):
        query_grads(i)

    for j in range(heads // 2):
        even = rot32[pl.ds(2 * j, tokens, stride=heads), :]
        odd = rot32[pl.ds(2 * j + 1, tokens, stride=heads), :]
        dqr_ref[:, pl.ds(j * 128, 128)] = jnp.where(
            low, even, pltpu.roll(odd, 64, 1)
        ).astype(jnp.bfloat16)

    c0 = add_context(0, n0, b0)
    c1 = add_context(1, n1, b1)
    finish(0, c0)
    for copy in [*forward.values(), *passed.values(), a0, a1, n0, n1, *b0, *b1, c0]:
        copy.wait_send()
    finish(1, c1)
    c1.wait_send()


def move(*refs):
    sources, targets, sem = refs[:4], refs[4:8], refs[8]
    rows = sources[0].shape[0] // PIECES
    copies = [
        pltpu.make_async_copy(
            sources[0].at[pl.ds(i * rows, rows)], targets[0].at[pl.ds(i * rows, rows)], sem.at[i]
        )
        for i in range(PIECES)
    ]
    copies += [
        pltpu.make_async_copy(sources[i], targets[i], sem.at[PIECES + i - 1]) for i in (1, 2, 3)
    ]
    for copy in copies:
        copy.start()
    for copy in copies:
        copy.wait()


def per_device(q_latent, q_rope, kv_latent, k_rope, out_grad, block_pos):
    tokens, heads, lat = q_latent.shape
    rows = tokens * heads
    keys = SPAN * tokens
    n_ctx = lax.axis_size("ctx")
    bf16, f32 = jnp.bfloat16, jnp.float32
    vmem = pl.BlockSpec(memory_space=pltpu.VMEM)
    hbm = pl.BlockSpec(memory_space=pltpu.HBM)
    widths = [width for _, width in SPLITS]

    def pairs(shape, kind):
        return [pltpu.VMEM(shape + (width,), kind) for width in widths]

    dma = pltpu.SemaphoreType.DMA
    scratch = [
        pltpu.SMEM(block_pos.shape, jnp.int32),
        pltpu.VMEM((tokens, lat), bf16),
        pltpu.VMEM((ROPE, tokens), bf16),
        pltpu.VMEM((tokens, heads * ROPE), bf16),
        pltpu.VMEM((SPAN, 2, 64, WIDE), bf16),
        pltpu.VMEM((rows, WIDE), bf16),
        pltpu.VMEM((rows, lat), bf16),
        pltpu.VMEM((rows, 128), f32),
        *[pltpu.VMEM((3 * keys // 4, CHUNK), f32) for _ in range(2)],
        *[pltpu.VMEM((keys, rows), f32) for _ in range(2)],
        *[pltpu.VMEM((8, rows), f32) for _ in range(2)],
        pltpu.VMEM((keys, rows), bf16),
        pltpu.VMEM((keys, rows), bf16),
        *pairs((2 * SPAN, 2, 32), f32),
        *pairs((2 * SPAN, 32), bf16),
        *pairs((2 * SPAN, 32), bf16),
        *pairs((3, 2, 32), bf16),
        *pairs((3, 2, 32), bf16),
        *pairs((32,), bf16),
        *pairs((32,), bf16),
        dma((6,)),
        dma((3,)), dma((3,)), dma((3,)), dma((3,)),
        dma((2, 2)), dma((2, 2)), dma((2, 3)), dma((2, 3)), dma((2,)), dma((2,)),
    ]
    macs = rows * keys * (WIDE * 3 + 2 * lat)
    dq, dqr, dkv, dkr = pl.pallas_call(
        functools.partial(kernel, n_ctx, heads),
        out_shape=(
            pltpu.VMEM((rows, lat), bf16),
            pltpu.VMEM((tokens, heads * ROPE), bf16),
            pltpu.VMEM((tokens // 4, lat), bf16),
            pltpu.VMEM((tokens // 4, ROPE), bf16),
        ),
        in_specs=[hbm] * 6,
        out_specs=(vmem,) * 4,
        scratch_shapes=scratch,
        compiler_params=pltpu.CompilerParams(
            collective_id=0, has_side_effects=True, vmem_limit_bytes=56 * 2**20
        ),
        cost_estimate=pl.CostEstimate(
            flops=2 * macs, bytes_accessed=7 * 2**20, transcendentals=rows * keys
        ),
    )(
        block_pos, kv_latent, k_rope.T, q_rope,
        q_latent.reshape(rows, lat), out_grad.reshape(rows, lat),
    )
    results = (dq, dqr, dkv, dkr)
    dq, dqr, dkv, dkr = pl.pallas_call(
        move,
        out_shape=tuple(jax.ShapeDtypeStruct(r.shape, r.dtype) for r in results),
        in_specs=[vmem] * 4,
        out_specs=(hbm,) * 4,
        scratch_shapes=[dma((PIECES + 3,))],
        compiler_params=pltpu.CompilerParams(vmem_limit_bytes=2**20),
    )(*results)
    return dq.reshape(tokens, heads, lat), dqr, dkv, dkr


def solution(mesh):
    in_specs = (
        P("ctx", "head", None),
        P("ctx", "head"),
        P("ctx", None),
        P("ctx", None),
        P("ctx", "head", None),
        P(),
    )
    out_specs = (
        P("ctx", "head", None),
        P("ctx", "head"),
        P(("ctx", "head"), None),
        P(("ctx", "head"), None),
    )
    return jax.shard_map(
        per_device, mesh=mesh, in_specs=in_specs, out_specs=out_specs, check_vma=False
    )
```

```python
import functools

import jax
import jax.numpy as jnp
from jax import lax
from jax.experimental import pallas as pl
from jax.experimental.pallas import tpu as pltpu
from jax.sharding import PartitionSpec as P

SPAN = 4
LAT = 512
ROPE = 64
WIDE = 640
SCALE = 192.0 ** (-0.5)
SCALE_LOG2 = SCALE * 1.4426950408889634
CHUNK = 256
ORDER = (0, 1, 3, 2)
PLACE = tuple(ORDER.index(k) for k in range(SPAN))
GROUPS = ((0, 1), (1, 3))
SPLITS = ((0, 256), (256, 384))

PIECES = 8

NT = (((1,), (1,)), ((), ()))
TN = (((0,), (0,)), ((), ()))


def dot(a, b, dims=(((1,), (0,)), ((), ()))):
    return lax.dot_general(a, b, dims, preferred_element_type=jnp.float32)


def kernel(
    n_ctx, heads,
    pos_hbm, kv_hbm, kr_hbm, qr_hbm, q_hbm, g_hbm,
    dq_ref, dqr_ref, dkv_ref, dkr_ref,
    block_pos, kv_ref, kr_ref, qr_ref, kvr, qv, gv, rot32, s_a, s_b, e_buf, dp_buf, tops, sums, ds_t, w_t,
    d0, d1, as0, as1, ar0, ar1, bs0, bs1, br0, br1, cs0, cs1, cr0, cr1,
    in_sem, f_send, f_recv, p_send, p_recv,
    a_send, a_recv, b_send, b_recv, c_send, c_recv,
):
    c = lax.axis_index("ctx")
    h = lax.axis_index("head")
    z = lax.div(h, 2)
    a = lax.rem(h, 2)
    sib = z * 2 + (1 - a)
    zpart = (1 - z) * 2 + a
    rows = qv.shape[0]
    half = rows // 2
    s_bufs = (s_a, s_b)

    def ctx_at(k):
        return lax.rem(c + k + n_ctx, n_ctx)

    load_keys = [
        pltpu.make_async_copy(kv_hbm, kv_ref, in_sem.at[0]),
        pltpu.make_async_copy(kr_hbm, kr_ref, in_sem.at[1]),
    ]
    load_rot = pltpu.make_async_copy(qr_hbm, qr_ref, in_sem.at[2])
    loads = [
        pltpu.make_async_copy(pos_hbm, block_pos, in_sem.at[3]),
        pltpu.make_async_copy(q_hbm, qv.at[:, pl.ds(0, LAT)], in_sem.at[4]),
        pltpu.make_async_copy(g_hbm, gv, in_sem.at[5]),
    ]
    barrier = pltpu.get_barrier_semaphore()
    peers = [(ctx_at(k), h) for k in (-3, -2, -1, 3, 2, 1)] + [(c, sib), (c, zpart)]
    for peer in peers:
        pl.semaphore_signal(barrier, inc=1, device_id=peer, device_id_type=pl.DeviceIdType.MESH)

    for load in [*load_keys, load_rot, *loads]:
        load.start()

    for load in load_keys:
        load.wait()
    kvr[0, :, :, pl.ds(0, LAT)] = kv_ref[...].reshape(2, 64, LAT)
    rot = kr_ref[...].astype(jnp.float32)
    kvr[0, :, :, pl.ds(LAT, 128)] = jnp.concatenate(
        [rot, jnp.zeros_like(rot)], axis=0
    ).T.astype(jnp.bfloat16).reshape(2, 64, 128)

    pl.semaphore_wait(barrier, len(peers))

    def remote(src, dst, send, recv, peer):
        return pltpu.make_async_remote_copy(
            src_ref=src, dst_ref=dst, send_sem=send, recv_sem=recv,
            device_id=peer, device_id_type=pl.DeviceIdType.MESH,
        )

    forward = {}
    for k in (1, 3, 2):
        forward[k] = remote(
            kvr.at[0, a], kvr.at[PLACE[k], a], f_send.at[k - 1], f_recv.at[k - 1], (ctx_at(k), h)
        )
        forward[k].start()

    load_rot.wait()
    tokens = qr_ref.shape[0]
    low = lax.broadcasted_iota(jnp.int32, (tokens, 128), 1) < ROPE
    for j in range(heads // 2):
        tile = qr_ref[:, pl.ds(j * 128, 128)].astype(jnp.float32)
        rot32[pl.ds(2 * j, tokens, stride=heads), :] = jnp.where(low, tile, 0.0)
        rot32[pl.ds(2 * j + 1, tokens, stride=heads), :] = jnp.where(
            low, pltpu.roll(tile, 64, 1), 0.0
        )
    qv[:, pl.ds(LAT, 128)] = rot32[...].astype(jnp.bfloat16)

    for load in loads:
        load.wait()
    passed = {}

    def pass_on(k):
        forward[k].wait_recv()
        passed[k] = remote(
            kvr.at[PLACE[k], a], kvr.at[PLACE[k], a], p_send.at[k - 1], p_recv.at[k - 1], (c, sib)
        )
        passed[k].start()

    key_pos = [
        block_pos[2 * ctx_at(-ORDER[slot // 2]) + slot % 2] for slot in range(2 * SPAN)
    ]
    query_pos = [block_pos[2 * c], block_pos[2 * c + 1]]
    lane_row = lax.broadcasted_iota(jnp.int32, (64, CHUNK), 1)
    sub_row = lax.broadcasted_iota(jnp.int32, (64, CHUNK), 0)
    chunks = rows // CHUNK

    def score(group, i):
        first, count = GROUPS[group]
        at = pl.ds(i * CHUNK, CHUNK)
        keys = kvr[pl.ds(first, count)].reshape(count * 128, WIDE)
        s_buf = s_bufs[i % 2]
        s_buf[pl.ds(0, count * 128), :] = dot(keys, qv[at, :], NT)
        dp_buf[pl.ds(first * 128, count * 128), at] = dot(keys[:, :LAT], gv[at, :], NT)

    def soften(group, i):
        first, count = GROUPS[group]
        at = pl.ds(i * CHUNK, CHUNK)
        s_buf = s_bufs[i % 2]
        second = i * CHUNK // half
        ahead = lax.div(lane_row + (i * CHUNK - second * half), heads) - sub_row
        top = jnp.full((1, CHUNK), -1e30, jnp.float32)
        hidden = []
        for j in range(2 * count):
            part = pl.ds(j * 64, 64)
            s = s_buf[part, :]
            if 2 * first + j == second:
                s = jnp.where(ahead >= 0, s, -jnp.inf)
                s_buf[part, :] = s
                hidden.append(0.0)
            else:
                hidden.append(
                    jnp.where(key_pos[2 * first + j] < query_pos[second], 0.0, jnp.inf)
                )
            top = jnp.maximum(top, jnp.max(s, axis=0, keepdims=True) - hidden[j])
        total = jnp.zeros((1, CHUNK), jnp.float32)
        for j in range(2 * count):
            e = jnp.exp2((s_buf[pl.ds(j * 64, 64), :] - (top + hidden[j])) * SCALE_LOG2)
            e_buf[pl.ds(first * 128 + j * 64, 64), at] = e
            total = total + jnp.sum(e, axis=0, keepdims=True)
        tops[pl.ds(group, 1), at] = top
        sums[pl.ds(group, 1), at] = total

    def join(i):
        at = pl.ds(i * CHUNK, CHUNK)
        parts = range(len(GROUPS))
        top_of = [tops[pl.ds(g, 1), at] for g in parts]
        top = functools.reduce(jnp.maximum, top_of)
        part_of = [jnp.exp2((t - top) * SCALE_LOG2) for t in top_of]
        total = sum(f * sums[pl.ds(g, 1), at] for g, f in zip(parts, part_of))
        inv = 1.0 / total
        factor = []
        for g in parts:
            factor += [part_of[g] * inv] * (2 * GROUPS[g][1])
        delta = jnp.zeros((1, CHUNK), jnp.float32)
        for slot in range(2 * SPAN):
            part = pl.ds(slot * 64, 64)
            w = (e_buf[part, at] * factor[slot]).astype(jnp.bfloat16)
            w_t[part, at] = w
            delta = delta + jnp.sum(
                w.astype(jnp.float32) * dp_buf[part, at], axis=0, keepdims=True
            )
        for slot in range(2 * SPAN):
            part = pl.ds(slot * 64, 64)
            ds_t[part, at] = (
                (e_buf[part, at] * factor[slot]) * (dp_buf[part, at] - delta)
            ).astype(jnp.bfloat16)

    score(0, 0)
    for i in range(chunks):
        if i == 5:
            pass_on(1)
            pass_on(3)
            pass_on(2)
        if i + 1 < chunks:
            score(0, i + 1)
        soften(0, i)
    passed[1].wait_recv()
    passed[3].wait_recv()
    passed[2].wait_recv()
    score(1, 0)
    for i in range(chunks):
        if i + 1 < chunks:
            score(1, i + 1)
        soften(1, i)
        join(i)

    d, asb, arb, bsb, brb = (d0, d1), (as0, as1), (ar0, ar1), (bs0, bs1), (br0, br1)
    csb, crb = (cs0, cs1), (cr0, cr1)

    def key_grads(n, first_place, count):
        first, width = SPLITS[n]
        at = pl.ds(first_place * 128, count * 128)
        slots = pl.ds(2 * first_place, 2 * count)
        shape = (2 * count, 2, 32)
        part = SCALE * dot(ds_t[at, :], qv[:, pl.ds(first, width)])
        latent = min(width, LAT - first)
        other = dot(w_t[at, :], gv[:, pl.ds(first, latent)])
        d[n][slots, :, :, pl.ds(0, latent)] = (part[:, :latent] + other).reshape(shape + (latent,))
        if latent < width:
            d[n][slots, :, :, pl.ds(latent, width - latent)] = part[:, latent:].reshape(
                shape + (width - latent,)
            )
        asb[n][slots] = d[n][slots, pl.ds(1 - a, 1)].reshape(2 * count, 32, width).astype(
            jnp.bfloat16
        )
        far = min(first_place, 1)
        copy = remote(
            asb[n].at[slots], arb[n].at[slots], a_send.at[n, far], a_recv.at[n, far], (c, sib)
        )
        copy.start()
        return copy

    def own(n, k):
        width = SPLITS[n][1]
        return d[n][pl.ds(2 * PLACE[k], 2), pl.ds(a, 1)].reshape(2, 32, width)

    def add_cores(n, copy):
        copy.wait_recv()
        sends = []
        for k in (2, 1, 3):
            got = arb[n][pl.ds(2 * PLACE[k], 2)].astype(jnp.float32)
            bsb[n][k - 1] = (own(n, k) + got).astype(jnp.bfloat16)
            sends.append(remote(
                bsb[n].at[k - 1], brb[n].at[k - 1], b_send.at[n, k - 1], b_recv.at[n, k - 1],
                (ctx_at(-k), h),
            ))
            sends[-1].start()
        return sends

    def add_context(n, near, sends):
        for copy in [near, *sends]:
            copy.wait_recv()
        added = own(n, 0) + arb[n][pl.ds(0, 2)].astype(jnp.float32)
        for k in (1, 2, 3):
            added = added + brb[n][k - 1].astype(jnp.float32)
        width = SPLITS[n][1]
        d[n][pl.ds(0, 2), pl.ds(a, 1)] = added.reshape(2, 1, 32, width)
        csb[n][...] = d[n][pl.ds(1 - z, 1), pl.ds(a, 1)].reshape(32, width).astype(jnp.bfloat16)
        copy = remote(csb[n], crb[n], c_send.at[n], c_recv.at[n], (c, zpart))
        copy.start()
        return copy

    def finish(n, copy):
        copy.wait_recv()
        first, width = SPLITS[n]
        result = d[n][pl.ds(z, 1), pl.ds(a, 1)].reshape(32, width) + crb[n][...].astype(jnp.float32)
        result = result.astype(jnp.bfloat16)
        latent = min(width, LAT - first)
        dkv_ref[:, pl.ds(first, latent)] = result[:, :latent]
        if latent < width:
            dkr_ref[...] = result[:, latent:latent + ROPE]

    def query_grads(i):
        start = i * CHUNK
        at = pl.ds(start, CHUNK)
        keys = kvr[...].reshape(SPAN * 128, WIDE)
        grad = SCALE * dot(ds_t[:, at], keys, TN)
        dq_ref[at, :] = grad[:, :LAT].astype(jnp.bfloat16)
        rot32[at, :] = grad[:, LAT:]

    a0 = key_grads(0, 1, 3)
    a1 = key_grads(1, 1, 3)
    b0 = add_cores(0, a0)
    n0 = key_grads(0, 0, 1)
    b1 = add_cores(1, a1)
    n1 = key_grads(1, 0, 1)
    for i in range(chunks):
        query_grads(i)

    for j in range(heads // 2):
        even = rot32[pl.ds(2 * j, tokens, stride=heads), :]
        odd = rot32[pl.ds(2 * j + 1, tokens, stride=heads), :]
        dqr_ref[:, pl.ds(j * 128, 128)] = jnp.where(
            low, even, pltpu.roll(odd, 64, 1)
        ).astype(jnp.bfloat16)

    c0 = add_context(0, n0, b0)
    c1 = add_context(1, n1, b1)
    finish(0, c0)
    for copy in [*forward.values(), *passed.values(), a0, a1, n0, n1, *b0, *b1, c0]:
        copy.wait_send()
    finish(1, c1)
    c1.wait_send()


def move(*refs):
    sources, targets, sem = refs[:4], refs[4:8], refs[8]
    rows = sources[0].shape[0] // PIECES
    copies = [
        pltpu.make_async_copy(
            sources[0].at[pl.ds(i * rows, rows)], targets[0].at[pl.ds(i * rows, rows)], sem.at[i]
        )
        for i in range(PIECES)
    ]
    copies += [
        pltpu.make_async_copy(sources[i], targets[i], sem.at[PIECES + i - 1]) for i in (1, 2, 3)
    ]
    for copy in copies:
        copy.start()
    for copy in copies:
        copy.wait()


def per_device(q_latent, q_rope, kv_latent, k_rope, out_grad, block_pos):
    tokens, heads, lat = q_latent.shape
    rows = tokens * heads
    keys = SPAN * tokens
    n_ctx = lax.axis_size("ctx")
    bf16, f32 = jnp.bfloat16, jnp.float32
    vmem = pl.BlockSpec(memory_space=pltpu.VMEM)
    hbm = pl.BlockSpec(memory_space=pltpu.HBM)
    widths = [width for _, width in SPLITS]

    def pairs(shape, kind):
        return [pltpu.VMEM(shape + (width,), kind) for width in widths]

    dma = pltpu.SemaphoreType.DMA
    scratch = [
        pltpu.SMEM(block_pos.shape, jnp.int32),
        pltpu.VMEM((tokens, lat), bf16),
        pltpu.VMEM((ROPE, tokens), bf16),
        pltpu.VMEM((tokens, heads * ROPE), bf16),
        pltpu.VMEM((SPAN, 2, 64, WIDE), bf16),
        pltpu.VMEM((rows, WIDE), bf16),
        pltpu.VMEM((rows, lat), bf16),
        pltpu.VMEM((rows, 128), f32),
        *[pltpu.VMEM((3 * keys // 4, CHUNK), f32) for _ in range(2)],
        *[pltpu.VMEM((keys, rows), f32) for _ in range(2)],
        *[pltpu.VMEM((8, rows), f32) for _ in range(2)],
        pltpu.VMEM((keys, rows), bf16),
        pltpu.VMEM((keys, rows), bf16),
        *pairs((2 * SPAN, 2, 32), f32),
        *pairs((2 * SPAN, 32), bf16),
        *pairs((2 * SPAN, 32), bf16),
        *pairs((3, 2, 32), bf16),
        *pairs((3, 2, 32), bf16),
        *pairs((32,), bf16),
        *pairs((32,), bf16),
        dma((6,)),
        dma((3,)), dma((3,)), dma((3,)), dma((3,)),
        dma((2, 2)), dma((2, 2)), dma((2, 3)), dma((2, 3)), dma((2,)), dma((2,)),
    ]
    macs = rows * keys * (WIDE * 3 + 2 * lat)
    dq, dqr, dkv, dkr = pl.pallas_call(
        functools.partial(kernel, n_ctx, heads),
        out_shape=(
            pltpu.VMEM((rows, lat), bf16),
            pltpu.VMEM((tokens, heads * ROPE), bf16),
            pltpu.VMEM((tokens // 4, lat), bf16),
            pltpu.VMEM((tokens // 4, ROPE), bf16),
        ),
        in_specs=[hbm] * 6,
        out_specs=(vmem,) * 4,
        scratch_shapes=scratch,
        compiler_params=pltpu.CompilerParams(
            collective_id=0, has_side_effects=True, vmem_limit_bytes=56 * 2**20
        ),
        cost_estimate=pl.CostEstimate(
            flops=2 * macs, bytes_accessed=7 * 2**20, transcendentals=rows * keys
        ),
    )(
        block_pos, kv_latent, k_rope.T, q_rope,
        q_latent.reshape(rows, lat), out_grad.reshape(rows, lat),
    )
    results = (dq, dqr, dkv, dkr)
    dq, dqr, dkv, dkr = pl.pallas_call(
        move,
        out_shape=tuple(jax.ShapeDtypeStruct(r.shape, r.dtype) for r in results),
        in_specs=[vmem] * 4,
        out_specs=(hbm,) * 4,
        scratch_shapes=[dma((PIECES + 3,))],
        compiler_params=pltpu.CompilerParams(vmem_limit_bytes=2**20),
    )(*results)
    return dq.reshape(tokens, heads, lat), dqr, dkv, dkr


def solution(mesh):
    in_specs = (
        P("ctx", "head", None),
        P("ctx", "head"),
        P("ctx", None),
        P("ctx", None),
        P("ctx", "head", None),
        P(),
    )
    out_specs = (
        P("ctx", "head", None),
        P("ctx", "head"),
        P(("ctx", "head"), None),
        P(("ctx", "head"), None),
    )
    return jax.shard_map(
        per_device, mesh=mesh, in_specs=in_specs, out_specs=out_specs, check_vma=False
    )
```

```python
import functools

import jax
import jax.numpy as jnp
from jax import lax
from jax.experimental import pallas as pl
from jax.experimental.pallas import tpu as pltpu
from jax.sharding import PartitionSpec as P

SPAN = 4
LAT = 512
ROPE = 64
WIDE = 640
SCALE = 192.0 ** (-0.5)
SCALE_LOG2 = SCALE * 1.4426950408889634
CHUNK = 256
ORDER = (0, 1, 3, 2)
PLACE = tuple(ORDER.index(k) for k in range(SPAN))
GROUPS = ((0, 1), (1, 3))
SPLITS = ((0, 256), (256, 384))

PIECES = 8

NT = (((1,), (1,)), ((), ()))
TN = (((0,), (0,)), ((), ()))


def dot(a, b, dims=(((1,), (0,)), ((), ()))):
    return lax.dot_general(a, b, dims, preferred_element_type=jnp.float32)


def kernel(
    n_ctx, heads,
    pos_hbm, kv_hbm, kr_hbm, qr_hbm, q_hbm, g_hbm,
    dq_ref, dqr_ref, dkv_ref, dkr_ref,
    block_pos, kv_ref, kr_ref, qr_ref, kvr, qv, gv, rot32, s_a, s_b, e_buf, dp_buf, tops, sums, ds_t, w_t,
    d0, d1, as0, as1, ar0, ar1, bs0, bs1, br0, br1, cs0, cs1, cr0, cr1,
    in_sem, f_send, f_recv, p_send, p_recv,
    a_send, a_recv, b_send, b_recv, c_send, c_recv,
):
    c = lax.axis_index("ctx")
    h = lax.axis_index("head")
    z = lax.div(h, 2)
    a = lax.rem(h, 2)
    sib = z * 2 + (1 - a)
    zpart = (1 - z) * 2 + a
    rows = qv.shape[0]
    half = rows // 2
    s_bufs = (s_a, s_b)

    def ctx_at(k):
        return lax.rem(c + k + n_ctx, n_ctx)

    load_keys = [
        pltpu.make_async_copy(kv_hbm, kv_ref, in_sem.at[0]),
        pltpu.make_async_copy(kr_hbm, kr_ref, in_sem.at[1]),
    ]
    load_rot = pltpu.make_async_copy(qr_hbm, qr_ref, in_sem.at[2])
    loads = [
        pltpu.make_async_copy(pos_hbm, block_pos, in_sem.at[3]),
        pltpu.make_async_copy(q_hbm, qv.at[:, pl.ds(0, LAT)], in_sem.at[4]),
        pltpu.make_async_copy(g_hbm, gv, in_sem.at[5]),
    ]
    barrier = pltpu.get_barrier_semaphore()
    peers = [(ctx_at(k), h) for k in (-3, -2, -1, 3, 2, 1)] + [(c, sib), (c, zpart)]
    for peer in peers:
        pl.semaphore_signal(barrier, inc=1, device_id=peer, device_id_type=pl.DeviceIdType.MESH)

    for load in [*load_keys, load_rot, *loads]:
        load.start()

    for load in load_keys:
        load.wait()
    kvr[0, :, :, pl.ds(0, LAT)] = kv_ref[...].reshape(2, 64, LAT)
    rot = kr_ref[...].astype(jnp.float32)
    kvr[0, :, :, pl.ds(LAT, 128)] = jnp.concatenate(
        [rot, jnp.zeros_like(rot)], axis=0
    ).T.astype(jnp.bfloat16).reshape(2, 64, 128)

    pl.semaphore_wait(barrier, len(peers))

    def remote(src, dst, send, recv, peer):
        return pltpu.make_async_remote_copy(
            src_ref=src, dst_ref=dst, send_sem=send, recv_sem=recv,
            device_id=peer, device_id_type=pl.DeviceIdType.MESH,
        )

    forward = {}
    for k in (2, 1, 3):
        forward[k] = remote(
            kvr.at[0, a], kvr.at[PLACE[k], a], f_send.at[k - 1], f_recv.at[k - 1], (ctx_at(k), h)
        )
        forward[k].start()

    load_rot.wait()
    tokens = qr_ref.shape[0]
    low = lax.broadcasted_iota(jnp.int32, (tokens, 128), 1) < ROPE
    for j in range(heads // 2):
        tile = qr_ref[:, pl.ds(j * 128, 128)].astype(jnp.float32)
        rot32[pl.ds(2 * j, tokens, stride=heads), :] = jnp.where(low, tile, 0.0)
        rot32[pl.ds(2 * j + 1, tokens, stride=heads), :] = jnp.where(
            low, pltpu.roll(tile, 64, 1), 0.0
        )
    qv[:, pl.ds(LAT, 128)] = rot32[...].astype(jnp.bfloat16)

    for load in loads:
        load.wait()
    passed = {}

    def pass_on(k):
        forward[k].wait_recv()
        passed[k] = remote(
            kvr.at[PLACE[k], a], kvr.at[PLACE[k], a], p_send.at[k - 1], p_recv.at[k - 1], (c, sib)
        )
        passed[k].start()

    key_pos = [
        block_pos[2 * ctx_at(-ORDER[slot // 2]) + slot % 2] for slot in range(2 * SPAN)
    ]
    query_pos = [block_pos[2 * c], block_pos[2 * c + 1]]
    lane_row = lax.broadcasted_iota(jnp.int32, (64, CHUNK), 1)
    sub_row = lax.broadcasted_iota(jnp.int32, (64, CHUNK), 0)
    chunks = rows // CHUNK

    def score(group, i):
        first, count = GROUPS[group]
        at = pl.ds(i * CHUNK, CHUNK)
        keys = kvr[pl.ds(first, count)].reshape(count * 128, WIDE)
        s_buf = s_bufs[i % 2]
        s_buf[pl.ds(0, count * 128), :] = dot(keys, qv[at, :], NT)
        dp_buf[pl.ds(first * 128, count * 128), at] = dot(keys[:, :LAT], gv[at, :], NT)

    def soften(group, i):
        first, count = GROUPS[group]
        at = pl.ds(i * CHUNK, CHUNK)
        s_buf = s_bufs[i % 2]
        second = i * CHUNK // half
        ahead = lax.div(lane_row + (i * CHUNK - second * half), heads) - sub_row
        top = jnp.full((1, CHUNK), -1e30, jnp.float32)
        hidden = []
        for j in range(2 * count):
            part = pl.ds(j * 64, 64)
            s = s_buf[part, :]
            if 2 * first + j == second:
                s = jnp.where(ahead >= 0, s, -jnp.inf)
                s_buf[part, :] = s
                hidden.append(0.0)
            else:
                hidden.append(
                    jnp.where(key_pos[2 * first + j] < query_pos[second], 0.0, jnp.inf)
                )
            top = jnp.maximum(top, jnp.max(s, axis=0, keepdims=True) - hidden[j])
        total = jnp.zeros((1, CHUNK), jnp.float32)
        for j in range(2 * count):
            e = jnp.exp2((s_buf[pl.ds(j * 64, 64), :] - (top + hidden[j])) * SCALE_LOG2)
            e_buf[pl.ds(first * 128 + j * 64, 64), at] = e
            total = total + jnp.sum(e, axis=0, keepdims=True)
        tops[pl.ds(group, 1), at] = top
        sums[pl.ds(group, 1), at] = total

    def join(i):
        at = pl.ds(i * CHUNK, CHUNK)
        parts = range(len(GROUPS))
        top_of = [tops[pl.ds(g, 1), at] for g in parts]
        top = functools.reduce(jnp.maximum, top_of)
        part_of = [jnp.exp2((t - top) * SCALE_LOG2) for t in top_of]
        total = sum(f * sums[pl.ds(g, 1), at] for g, f in zip(parts, part_of))
        inv = 1.0 / total
        factor = []
        for g in parts:
            factor += [part_of[g] * inv] * (2 * GROUPS[g][1])
        delta = jnp.zeros((1, CHUNK), jnp.float32)
        for slot in range(2 * SPAN):
            part = pl.ds(slot * 64, 64)
            w = (e_buf[part, at] * factor[slot]).astype(jnp.bfloat16)
            w_t[part, at] = w
            delta = delta + jnp.sum(
                w.astype(jnp.float32) * dp_buf[part, at], axis=0, keepdims=True
            )
        for slot in range(2 * SPAN):
            part = pl.ds(slot * 64, 64)
            ds_t[part, at] = (
                (e_buf[part, at] * factor[slot]) * (dp_buf[part, at] - delta)
            ).astype(jnp.bfloat16)

    score(0, 0)
    for i in range(chunks):
        if i == 5:
            pass_on(1)
            pass_on(3)
            pass_on(2)
        if i + 1 < chunks:
            score(0, i + 1)
        soften(0, i)
    passed[1].wait_recv()
    passed[3].wait_recv()
    passed[2].wait_recv()
    score(1, 0)
    for i in range(chunks):
        if i + 1 < chunks:
            score(1, i + 1)
        soften(1, i)
        join(i)

    d, asb, arb, bsb, brb = (d0, d1), (as0, as1), (ar0, ar1), (bs0, bs1), (br0, br1)
    csb, crb = (cs0, cs1), (cr0, cr1)

    def key_grads(n, first_place, count):
        first, width = SPLITS[n]
        at = pl.ds(first_place * 128, count * 128)
        slots = pl.ds(2 * first_place, 2 * count)
        shape = (2 * count, 2, 32)
        part = SCALE * dot(ds_t[at, :], qv[:, pl.ds(first, width)])
        latent = min(width, LAT - first)
        other = dot(w_t[at, :], gv[:, pl.ds(first, latent)])
        d[n][slots, :, :, pl.ds(0, latent)] = (part[:, :latent] + other).reshape(shape + (latent,))
        if latent < width:
            d[n][slots, :, :, pl.ds(latent, width - latent)] = part[:, latent:].reshape(
                shape + (width - latent,)
            )
        asb[n][slots] = d[n][slots, pl.ds(1 - a, 1)].reshape(2 * count, 32, width).astype(
            jnp.bfloat16
        )
        far = min(first_place, 1)
        copy = remote(
            asb[n].at[slots], arb[n].at[slots], a_send.at[n, far], a_recv.at[n, far], (c, sib)
        )
        copy.start()
        return copy

    def own(n, k):
        width = SPLITS[n][1]
        return d[n][pl.ds(2 * PLACE[k], 2), pl.ds(a, 1)].reshape(2, 32, width)

    def add_cores(n, copy):
        copy.wait_recv()
        sends = []
        for k in (2, 1, 3):
            got = arb[n][pl.ds(2 * PLACE[k], 2)].astype(jnp.float32)
            bsb[n][k - 1] = (own(n, k) + got).astype(jnp.bfloat16)
            sends.append(remote(
                bsb[n].at[k - 1], brb[n].at[k - 1], b_send.at[n, k - 1], b_recv.at[n, k - 1],
                (ctx_at(-k), h),
            ))
            sends[-1].start()
        return sends

    def add_context(n, near, sends):
        for copy in [near, *sends]:
            copy.wait_recv()
        added = own(n, 0) + arb[n][pl.ds(0, 2)].astype(jnp.float32)
        for k in (1, 2, 3):
            added = added + brb[n][k - 1].astype(jnp.float32)
        width = SPLITS[n][1]
        d[n][pl.ds(0, 2), pl.ds(a, 1)] = added.reshape(2, 1, 32, width)
        csb[n][...] = d[n][pl.ds(1 - z, 1), pl.ds(a, 1)].reshape(32, width).astype(jnp.bfloat16)
        copy = remote(csb[n], crb[n], c_send.at[n], c_recv.at[n], (c, zpart))
        copy.start()
        return copy

    def finish(n, copy):
        copy.wait_recv()
        first, width = SPLITS[n]
        result = d[n][pl.ds(z, 1), pl.ds(a, 1)].reshape(32, width) + crb[n][...].astype(jnp.float32)
        result = result.astype(jnp.bfloat16)
        latent = min(width, LAT - first)
        dkv_ref[:, pl.ds(first, latent)] = result[:, :latent]
        if latent < width:
            dkr_ref[...] = result[:, latent:latent + ROPE]

    def query_grads(i):
        start = i * CHUNK
        at = pl.ds(start, CHUNK)
        keys = kvr[...].reshape(SPAN * 128, WIDE)
        grad = SCALE * dot(ds_t[:, at], keys, TN)
        dq_ref[at, :] = grad[:, :LAT].astype(jnp.bfloat16)
        rot32[at, :] = grad[:, LAT:]

    a0 = key_grads(0, 1, 3)
    a1 = key_grads(1, 1, 3)
    b0 = add_cores(0, a0)
    n0 = key_grads(0, 0, 1)
    b1 = add_cores(1, a1)
    n1 = key_grads(1, 0, 1)
    for i in range(chunks):
        query_grads(i)

    for j in range(heads // 2):
        even = rot32[pl.ds(2 * j, tokens, stride=heads), :]
        odd = rot32[pl.ds(2 * j + 1, tokens, stride=heads), :]
        dqr_ref[:, pl.ds(j * 128, 128)] = jnp.where(
            low, even, pltpu.roll(odd, 64, 1)
        ).astype(jnp.bfloat16)

    c0 = add_context(0, n0, b0)
    c1 = add_context(1, n1, b1)
    finish(0, c0)
    for copy in [*forward.values(), *passed.values(), a0, a1, n0, n1, *b0, *b1, c0]:
        copy.wait_send()
    finish(1, c1)
    c1.wait_send()


def move(*refs):
    sources, targets, sem = refs[:4], refs[4:8], refs[8]
    rows = sources[0].shape[0] // PIECES
    copies = [
        pltpu.make_async_copy(
            sources[0].at[pl.ds(i * rows, rows)], targets[0].at[pl.ds(i * rows, rows)], sem.at[i]
        )
        for i in range(PIECES)
    ]
    copies += [
        pltpu.make_async_copy(sources[i], targets[i], sem.at[PIECES + i - 1]) for i in (1, 2, 3)
    ]
    for copy in copies:
        copy.start()
    for copy in copies:
        copy.wait()


def per_device(q_latent, q_rope, kv_latent, k_rope, out_grad, block_pos):
    tokens, heads, lat = q_latent.shape
    rows = tokens * heads
    keys = SPAN * tokens
    n_ctx = lax.axis_size("ctx")
    bf16, f32 = jnp.bfloat16, jnp.float32
    vmem = pl.BlockSpec(memory_space=pltpu.VMEM)
    hbm = pl.BlockSpec(memory_space=pltpu.HBM)
    widths = [width for _, width in SPLITS]

    def pairs(shape, kind):
        return [pltpu.VMEM(shape + (width,), kind) for width in widths]

    dma = pltpu.SemaphoreType.DMA
    scratch = [
        pltpu.SMEM(block_pos.shape, jnp.int32),
        pltpu.VMEM((tokens, lat), bf16),
        pltpu.VMEM((ROPE, tokens), bf16),
        pltpu.VMEM((tokens, heads * ROPE), bf16),
        pltpu.VMEM((SPAN, 2, 64, WIDE), bf16),
        pltpu.VMEM((rows, WIDE), bf16),
        pltpu.VMEM((rows, lat), bf16),
        pltpu.VMEM((rows, 128), f32),
        *[pltpu.VMEM((3 * keys // 4, CHUNK), f32) for _ in range(2)],
        *[pltpu.VMEM((keys, rows), f32) for _ in range(2)],
        *[pltpu.VMEM((8, rows), f32) for _ in range(2)],
        pltpu.VMEM((keys, rows), bf16),
        pltpu.VMEM((keys, rows), bf16),
        *pairs((2 * SPAN, 2, 32), f32),
        *pairs((2 * SPAN, 32), bf16),
        *pairs((2 * SPAN, 32), bf16),
        *pairs((3, 2, 32), bf16),
        *pairs((3, 2, 32), bf16),
        *pairs((32,), bf16),
        *pairs((32,), bf16),
        dma((6,)),
        dma((3,)), dma((3,)), dma((3,)), dma((3,)),
        dma((2, 2)), dma((2, 2)), dma((2, 3)), dma((2, 3)), dma((2,)), dma((2,)),
    ]
    macs = rows * keys * (WIDE * 3 + 2 * lat)
    dq, dqr, dkv, dkr = pl.pallas_call(
        functools.partial(kernel, n_ctx, heads),
        out_shape=(
            pltpu.VMEM((rows, lat), bf16),
            pltpu.VMEM((tokens, heads * ROPE), bf16),
            pltpu.VMEM((tokens // 4, lat), bf16),
            pltpu.VMEM((tokens // 4, ROPE), bf16),
        ),
        in_specs=[hbm] * 6,
        out_specs=(vmem,) * 4,
        scratch_shapes=scratch,
        compiler_params=pltpu.CompilerParams(
            collective_id=0, has_side_effects=True, vmem_limit_bytes=56 * 2**20
        ),
        cost_estimate=pl.CostEstimate(
            flops=2 * macs, bytes_accessed=7 * 2**20, transcendentals=rows * keys
        ),
    )(
        block_pos, kv_latent, k_rope.T, q_rope,
        q_latent.reshape(rows, lat), out_grad.reshape(rows, lat),
    )
    results = (dq, dqr, dkv, dkr)
    dq, dqr, dkv, dkr = pl.pallas_call(
        move,
        out_shape=tuple(jax.ShapeDtypeStruct(r.shape, r.dtype) for r in results),
        in_specs=[vmem] * 4,
        out_specs=(hbm,) * 4,
        scratch_shapes=[dma((PIECES + 3,))],
        compiler_params=pltpu.CompilerParams(vmem_limit_bytes=2**20),
    )(*results)
    return dq.reshape(tokens, heads, lat), dqr, dkv, dkr


def solution(mesh):
    in_specs = (
        P("ctx", "head", None),
        P("ctx", "head"),
        P("ctx", None),
        P("ctx", None),
        P("ctx", "head", None),
        P(),
    )
    out_specs = (
        P("ctx", "head", None),
        P("ctx", "head"),
        P(("ctx", "head"), None),
        P(("ctx", "head"), None),
    )
    return jax.shard_map(
        per_device, mesh=mesh, in_specs=in_specs, out_specs=out_specs, check_vma=False
    )
```
